512 devices in a mesh: seq: 32 (over y, x), head: 16 (over z, core).
Axes of the slice: x: 4, y: 8, z: 8, core: 2. Of those that a mesh axis runs over, the one named last changes fastest.
Arguments:
- queries: bfloat16 [65536, 128], P('seq', 'head'), may hold values from -0.1875 to 0.1875
- key_vectors: bfloat16 [65536, 128], P('seq', 'head'), may hold values from -0.1875 to 0.1875
- values: bfloat16 [65536, 4096], P('seq', 'head'), may hold values from -6 to 6
- level_table: float32 [8, 17], replicated, may hold values from 0.25 to 2.5
- level_class: int32 [65536], P('seq'), may hold values from 0 to 7
- doc_ids: int32 [65536], P('seq'), may hold values from 0 to 2, never falling along the last dimension, each value on 1 to 33792 neighbouring positions
Outputs:
- mixed: bfloat16 [65536, 4096], P('seq', 'head')
The draws below stay inside these ranges and needn't reach their ends.
Inputs may be any that keep to these rules, and one draw needn't show every extreme that they name: `doc_ids`: document numbers never fall along the window; each document is one run of tokens, the longest exactly 33792 tokens.
All inputs are finite; a program needn't handle non-finite values.
Results may differ from the reference program's by a relative error of at most 0.013.
Values may be sent and summed in bfloat16 or wider, within the bound.
A program may use at most 64 MiB of HBM per device.

```python
import math
import jax
import jax.numpy as jnp
import numpy as np
from jax import lax

TOK_DEV = 2048
QK = 128
V_HEADS = 32
HEAD = 128
TABLE_ROWS = 8
LEVELS = 17
TOKENS = 65536


def with_ends(result, rng, least, largest):
    index_at = [jax.random.randint(jax.random.fold_in(rng, axis), (), 0, length) for axis, length in enumerate(result.shape)]
    longest = result.shape.index(max(result.shape))
    beside = index_at[:longest] + [(index_at[longest] + 1) % result.shape[longest]] + index_at[longest + 1:]
    return result.at[tuple(index_at)].set(least).at[tuple(beside)].set(largest)


def block_levels(key, dims, pieces, smallest, high):
    loudness = 1.0
    for dim, parts in pieces:
        steps = jax.random.uniform(jax.random.fold_in(jax.random.fold_in(key, 6), dim), (parts,), jnp.float32, smallest / len(pieces), high / len(pieces))
        loudness = loudness * jnp.repeat(jnp.exp(steps), dims[dim] // parts).reshape((-1,) + (1,) * (len(dims) - 1 - dim))
    return loudness


def profile(number_of, total, bound, lean):
    weights = [(1 << 20) // math.isqrt(rank ** lean) + 1 for rank in range(2, number_of + 1)]
    spare, given = total - bound - (number_of - 1), [1] * (number_of - 1)
    while spare > 0:
        candidates = [i for i in range(number_of - 1) if given[i] < bound]
        pool, left = sum([weights[i] for i in candidates]), spare
        for i in candidates:
            more = min(bound - given[i], max(1, left * weights[i] // pool), spare)
            given[i] = given[i] + more
            spare = spare - more
    return np.array([bound] + given)


def uneven_parts(own_key, amount, total, most, slope):
    if amount == 2:
        one = jax.random.randint(own_key, (), max(1, total - most), min(most, total - 1) + 1)
        return jnp.stack([one, total - one])
    tallies = jnp.asarray(profile(amount, total, most, slope), jnp.int32)
    pairs = (amount - 1) // 2
    giver, sink = tallies[1:1 + 2 * pairs:2], tallies[2:2 + 2 * pairs:2]
    room = jnp.minimum(giver - 1, most - sink)
    shifted = jax.random.randint(jax.random.fold_in(own_key, 1), (pairs,), 0, 1 << 20) % (room + 1)
    tallies = tallies.at[1:1 + 2 * pairs:2].set(giver - shifted).at[2:2 + 2 * pairs:2].set(sink + shifted)
    return tallies[jax.random.permutation(jax.random.fold_in(own_key, 2), amount)]


def noise(stream_key, shape, width, limit, cuts=(), kind=jnp.bfloat16):
    values = width * jax.random.normal(stream_key, shape, jnp.float32)
    if cuts:
        values = values * block_levels(stream_key, shape, cuts, -0.22, 0.18)
    return jnp.clip(values, -limit, limit).astype(kind)


def setup_inputs(seed: int = 0) -> dict:
    arg_keys = jax.random.split(jax.random.key(seed), 7)
    return {
        "queries": noise(arg_keys[0], (TOKENS, QK), 0.03, 0.1875, ((0, 32), (1, 16))),
        "key_vectors": noise(arg_keys[1], (TOKENS, QK), 0.03, 0.1875, ((0, 32), (1, 16))),
        "values": noise(arg_keys[2], (TOKENS, V_HEADS * HEAD), 1.0, 6.0, ((0, 32), (1, 16))),
        "level_table": jnp.clip(jnp.exp(jax.random.uniform(arg_keys[3], (TABLE_ROWS, LEVELS), jnp.float32, math.log(0.25), math.log(2.5))), 0.25, 2.5),
        "level_class": with_ends(jax.random.randint(arg_keys[4], (TOKENS,), 0, TABLE_ROWS), jax.random.fold_in(arg_keys[4], 1), 0, TABLE_ROWS - 1).astype(jnp.int32),
        "doc_ids": jnp.searchsorted(jnp.cumsum(uneven_parts(arg_keys[5], 3, TOKENS, TOKENS // 2 + TOK_DEV // 2, 0)), jnp.arange(TOKENS), side="right").astype(jnp.int32),
    }


def bit_length(number):
    total = jnp.zeros_like(number)
    for shift in range(31):
        total = total + (number >= (1 << shift)).astype(jnp.int32)
    return total


def reference(queries, key_vectors, values, level_table, level_class, doc_ids):
    block_count = queries.shape[0] // TOK_DEV
    seq_bits = block_count.bit_length() - 1
    key_width = queries.shape[1]
    value_width = values.shape[1]
    base_level = TOK_DEV.bit_length()
    level_weights = jnp.take(level_table, level_class, axis=0)
    q_blocks = queries.reshape(block_count, TOK_DEV, key_width)
    k_blocks = key_vectors.reshape(block_count, TOK_DEV, key_width)
    v_blocks = values.reshape(block_count, TOK_DEV, value_width)
    w_blocks = level_weights.reshape(block_count, TOK_DEV, level_table.shape[1])
    d_blocks = doc_ids.reshape(block_count, TOK_DEV)
    last_docs = d_blocks[:, TOK_DEV - 1]

    def tail_of(block):
        keys_here, vals_here, docs_here = block
        kept = jnp.where((docs_here == docs_here[TOK_DEV - 1])[:, None], vals_here, jnp.zeros_like(vals_here))
        return jnp.dot(keys_here.T, kept, preferred_element_type=jnp.float32)

    tails = lax.map(tail_of, (k_blocks, v_blocks, d_blocks))
    local_pos = jnp.arange(TOK_DEV, dtype=jnp.int32)
    level_ids = bit_length(local_pos[:, None] ^ local_pos[None, :])
    causal = local_pos[None, :] <= local_pos[:, None]
    block_ids = jnp.arange(block_count, dtype=jnp.int32)

    def one_block(block):
        position, q_here, k_here, v_here, w_here, d_here = block
        scores = jnp.dot(q_here, k_here.T, preferred_element_type=jnp.float32)
        weight_grid = jnp.take_along_axis(w_here, level_ids, axis=1)
        allowed = causal & (d_here[:, None] == d_here[None, :])
        weighted = jnp.where(allowed, weight_grid * scores, 0.0).astype(jnp.bfloat16)
        near = jnp.dot(weighted, v_here, preferred_element_type=jnp.float32)
        picks = []
        for level_bit in range(seq_bits):
            lowest = (position >> (level_bit + 1)) << (level_bit + 1)
            inside = (((position >> level_bit) & 1) == 1) & (block_ids >= lowest) & (block_ids < lowest + (1 << level_bit)) & (last_docs == d_here[0])
            picks.append(inside.astype(jnp.float32))
        select = jnp.stack(picks)
        buckets = jnp.einsum("bj,jch->bch", select, tails, precision=lax.Precision.HIGHEST)
        far_weights = w_here[:, base_level:base_level + seq_bits]
        weighted_q = (far_weights[:, :, None] * q_here.astype(jnp.float32)[:, None, :]).reshape(TOK_DEV, seq_bits * key_width)
        far = jnp.dot(weighted_q, buckets.reshape(seq_bits * key_width, value_width), precision=lax.Precision.HIGHEST)
        far = jnp.where((d_here == d_here[0])[:, None], far, 0.0)
        return (near + far).astype(jnp.bfloat16)

    mixed = lax.map(one_block, (block_ids, q_blocks, k_blocks, v_blocks, w_blocks, d_blocks))
    return mixed.reshape(queries.shape[0], value_width)
```

```python
import jax
import jax.numpy as jnp
from jax import lax
from jax.experimental import pallas as pl
from jax.experimental.pallas import tpu as pltpu
from jax.sharding import PartitionSpec as P

MESH = pl.DeviceIdType.MESH
F32 = jnp.float32
BF16 = jnp.bfloat16

X = 4
Y = 8
Z = 8
TILE = 256
NT = 8
HALF = 128
WIDTH = 256
NEAR_LEVELS = 9
MID_LEVELS = 3
FAR_LEVELS = 5
QROWS = 32
TAGGED = QROWS + 16
Z_ORDER = (4, 3, 5, 2, 6, 1, 7)
DIM0 = (((0,), (0,)), ((), ()))


def dot(a, b):
    return jnp.dot(a, b, preferred_element_type=F32)


def same(a, b):
    return jnp.where(a == b, 1.0, 0.0).astype(F32)


def body(
    k_hbm,
    q_hbm,
    v_hbm,
    tab_ref,
    cls_ref,
    doc_ref,
    out_ref,
    k8,
    q8,
    v,
    kg,
    qg,
    onehot,
    table,
    grid,
    kt,
    state,
    left9,
    left10,
    left11,
    tails,
    xbuf,
    xlow,
    xout,
    ysend,
    ybuf,
    ylow,
    yout,
    ymask,
    bucket,
    qw,
    near,
    in_sem,
    ks_sem,
    kr_sem,
    kps_sem,
    kpr_sem,
    qs_sem,
    qr_sem,
    qps_sem,
    qpr_sem,
    xs_sem,
    xr_sem,
    as_sem,
    ar_sem,
    ys_sem,
    yr_sem,
    bs_sem,
    br_sem,
):
    seq = lax.axis_index("seq")
    head = lax.axis_index("head")
    x = seq % X
    y = seq // X
    z = head // 2
    c = head % 2

    def at_z(d):
        return {"seq": seq, "head": ((z + d) % Z) * 2 + c}

    def at_x(d):
        return {"seq": y * X + (x + d) % X, "head": head}

    def at_y(row):
        return {"seq": row * X + x, "head": head}

    partner = {"seq": seq, "head": z * 2 + (1 - c)}

    def remote(src, dst, send, recv, device):
        return pltpu.make_async_remote_copy(
            src_ref=src,
            dst_ref=dst,
            send_sem=send,
            recv_sem=recv,
            device_id=device,
            device_id_type=MESH,
        )

    load_k = pltpu.make_async_copy(k_hbm, k8, in_sem.at[0])
    load_q = pltpu.make_async_copy(q_hbm, q8, in_sem.at[1])
    load_v = pltpu.make_async_copy(v_hbm, v, in_sem.at[2])
    load_k.start()
    load_q.start()
    load_v.start()

    barrier = pltpu.get_barrier_semaphore()
    peers = [at_z(d) for d in range(1, Z)] + [at_x(d) for d in range(1, X)]
    peers = peers + [at_y((y + d) % Y) for d in range(1, Y)] + [partner]
    for peer in peers:
        pl.semaphore_signal(barrier, inc=1, device_id=peer, device_id_type=MESH)

    def pack(shard):
        wide = shard[...].astype(F32)
        return jnp.concatenate([wide[:, :1024], wide[:, 1024:]], axis=0).astype(BF16)

    load_k.wait()
    kg[c, z] = pack(k8)
    load_q.wait()
    qg[c, z] = pack(q8)
    pl.semaphore_wait(barrier, len(peers))

    k_copies = {}
    q_copies = {}
    for d in Z_ORDER:
        k_copies[d] = remote(kg.at[c, z], kg.at[c, z], ks_sem.at[d], kr_sem.at[d], at_z(d))
        k_copies[d].start()

    def k_partner(d):
        slot = kg.at[c, (z + Z - d) % Z]
        return remote(slot, slot, kps_sem.at[d], kpr_sem.at[d], partner)

    k_partner(0).start()
    for d in Z_ORDER:
        q_copies[d] = remote(qg.at[c, z], qg.at[c, z], qs_sem.at[d], qr_sem.at[d], at_z(d))
        q_copies[d].start()

    for order, level in enumerate(list(range(NEAR_LEVELS)) + [None] + list(range(NEAR_LEVELS, 17))):
        columns = slice(order * HALF, (order + 1) * HALF)
        if level is None:
            row = lax.broadcasted_iota(jnp.int32, (32, HALF), 0)
            table[:, columns] = jnp.where(row == 24, 1.0, 0.0).astype(BF16)
        else:
            weight = jnp.broadcast_to(tab_ref[:, level : level + 1], (8, HALF))
            high = weight.astype(BF16).astype(F32)
            middle = (weight - high).astype(BF16).astype(F32)
            low = weight - high - middle
            parts = [high, middle, low, jnp.zeros_like(low)]
            table[:, columns] = jnp.concatenate(parts, axis=0).astype(BF16)

    def doc_row(block):
        return doc_ref[pl.ds(block, 1), :].astype(F32)

    def doc_tile(i):
        return jnp.concatenate([doc_row(2 * i), doc_row(2 * i + 1)], axis=1)

    first_doc = doc_ref[0:1, 0:1].astype(F32)

    def last_doc(i):
        return doc_ref[2 * i + 1 : 2 * i + 2, HALF - 1 : HALF].astype(F32)

    @pl.loop(0, NT)
    def _(i):
        row8 = lax.broadcasted_iota(jnp.int32, (8, TILE), 0)
        classes = jnp.concatenate(
            [cls_ref[pl.ds(2 * i, 1), :], cls_ref[pl.ds(2 * i + 1, 1), :]], axis=1
        )
        hot = jnp.where(row8 == classes, 1.0, 0.0).astype(F32)
        docs = jnp.where(row8 == 0, doc_tile(i), 0.0)
        onehot[i] = jnp.concatenate([hot, hot, hot, docs], axis=0).astype(BF16)
        wide = lax.dot_general(
            onehot[i], table[:, : 10 * HALF], DIM0, preferred_element_type=F32
        )
        t_pos = lax.broadcasted_iota(jnp.int32, (HALF, HALF), 0)
        s_pos = lax.broadcasted_iota(jnp.int32, (HALF, HALF), 1)
        apart = t_pos ^ s_pos
        causal = s_pos <= t_pos
        for a in range(2):
            rows = slice(a * HALF, (a + 1) * HALF)
            doc_t = wide[rows, 9 * HALF : 10 * HALF]
            weight = wide[rows, :HALF]
            for level in range(1, 8):
                column = wide[rows, level * HALF : (level + 1) * HALF]
                weight = jnp.where(apart >= 1 << (level - 1), column, weight)
            allowed = causal & (doc_t == doc_row(2 * i + a))
            grid[i, rows, rows] = jnp.where(allowed, weight, 0.0)
            if a == 1:
                weight = wide[rows, 8 * HALF : 9 * HALF]
                grid[i, rows, :HALF] = jnp.where(doc_t == doc_row(2 * i), weight, 0.0)
            else:
                grid[i, rows, HALF:] = jnp.zeros((HALF, HALF), F32)

    ylow[...] = jnp.zeros_like(ylow)
    ymask[...] = jnp.zeros_like(ymask)
    load_v.wait()

    for d in (1, 7, 2, 6, 3, 5, 4):
        k_copies[d].wait_recv()
        k_partner(d).start()
    for d in (0, 1, 7, 2, 6, 3, 5, 4):
        k_partner(d).wait_recv()

    def unpacked(gathered, j):
        wide = gathered[:, :, :, pl.ds(pl.multiple_of(j * TILE, TILE), TILE)].astype(F32)
        return [wide[:, :, 8 * a : 8 * a + 8, :].reshape(HALF, TILE) for a in range(2)]

    @pl.loop(0, NT // 2)
    def _(j):
        for a, keys in enumerate(unpacked(kg, j)):
            i = a * (NT // 2) + j
            docs = doc_tile(i)
            kept = jnp.where(docs == docs[:, TILE - 1 : TILE], keys, 0.0)
            kt[i] = keys.astype(BF16)
            part = dot(kept.astype(BF16), v[pl.ds(pl.multiple_of(i * TILE, TILE), TILE), :])
            state[i] = part
            left9[i] = part.astype(BF16)

    level_states = [state[i] for i in range(NT)]
    pairs = [
        level_states[2 * j + 1] + same(last_doc(2 * j), last_doc(2 * j + 1)) * level_states[2 * j]
        for j in range(4)
    ]
    for j in range(4):
        left10[j] = pairs[j].astype(BF16)
    quads = [
        pairs[2 * j + 1] + same(last_doc(4 * j + 1), last_doc(4 * j + 3)) * pairs[2 * j]
        for j in range(2)
    ]
    left11[...] = quads[0].astype(BF16)
    tail = quads[1] + same(last_doc(3), last_doc(7)) * quads[0]
    tag = jnp.broadcast_to(last_doc(7), (16, WIDTH)).astype(BF16)
    for p in range(X):
        tails[p, :QROWS] = tail[p * QROWS : (p + 1) * QROWS].astype(BF16)
        tails[p, QROWS:] = tag

    x_copies = {}
    for d in (2, 1, 3):
        x_copies[d] = remote(
            tails.at[(x + d) % X], xbuf.at[x], xs_sem.at[d], xr_sem.at[d], at_x(d)
        )
        x_copies[d].start()
    xbuf[x] = tails[x]

    for d in Z_ORDER:
        q_copies[d].wait_recv()
    q_partner = remote(qg.at[c], qg.at[c], qps_sem.at[0], qpr_sem.at[0], partner)
    q_partner.start()

    for d in (1, 3, 2):
        x_copies[d].wait_recv()
    ends = [xbuf[p, QROWS:].astype(F32)[0:1, 0:1] for p in range(X)]
    terms = [xbuf[p, :QROWS].astype(F32) for p in range(X)]
    low_pair = terms[1] + same(ends[0], ends[1]) * terms[0]
    high_pair = terms[3] + same(ends[2], ends[3]) * terms[2]
    row_tail = high_pair + same(ends[1], ends[3]) * low_pair
    ysend[:QROWS] = row_tail.astype(BF16)
    ysend[QROWS:] = jnp.broadcast_to(ends[3], (16, WIDTH)).astype(BF16)

    def y_copy(d):
        return remote(ysend, ybuf.at[y], ys_sem.at[d], yr_sem.at[d], at_y((y + d) % Y))

    for d in (4, 3, 5, 2, 6, 1, 7):

        @pl.when(y + d < Y)
        def _():
            y_copy(d).start()

    blank = jnp.zeros((QROWS, WIDTH), BF16)
    xlow[0, :QROWS] = blank
    xlow[0, QROWS:] = blank
    xlow[1, :QROWS] = xbuf[0, :QROWS]
    xlow[1, QROWS:] = blank
    xlow[2, :QROWS] = blank
    xlow[2, QROWS:] = low_pair.astype(BF16)
    xlow[3, :QROWS] = xbuf[2, :QROWS]
    xlow[3, QROWS:] = low_pair.astype(BF16)
    a_copies = {}
    for d in (2, 1, 3):
        a_copies[d] = remote(
            xlow.at[(x + d) % X], xout.at[x], as_sem.at[d], ar_sem.at[d], at_x(d)
        )
        a_copies[d].start()
    xout[x] = xlow[x]

    q_partner.wait_recv()

    def near_tile(i, queries):
        turned = queries.T
        rows = pl.ds(pl.multiple_of(i * TILE, TILE), TILE)
        scores = dot(turned.astype(BF16), kt[i])
        weighted = (scores * grid[i]).astype(BF16)
        total = dot(weighted, v[rows, :])
        wide = lax.dot_general(
            onehot[i], table[:, 9 * HALF :], DIM0, preferred_element_type=F32
        )
        doc_t = wide[:, :HALF]
        mids = []
        for b in range(MID_LEVELS):
            end = jnp.maximum((i >> b << b) - 1, 0)
            end_doc = doc_row(2 * end + 1)[:, HALF - 1 : HALF]
            present = jnp.where((i >> b) % 2 == 1, 1.0, 0.0).astype(F32)
            weight = jnp.where(doc_t == end_doc, wide[:, (1 + b) * HALF : (2 + b) * HALF], 0.0)
            mids.append((weight * (turned * present)).astype(BF16))
        lefts = [
            left9[jnp.maximum(i - 1, 0)],
            left10[jnp.maximum((i >> 1) - 1, 0)],
            left11[...],
        ]
        total = total + dot(jnp.concatenate(mids, axis=1), jnp.concatenate(lefts, axis=0))
        near[i] = total
        kept = jnp.where(doc_t == first_doc, turned, 0.0)
        for b in range(FAR_LEVELS):
            start = (1 + MID_LEVELS + b) * HALF
            qw[i, :, b * HALF : (b + 1) * HALF] = (wide[:, start : start + HALF] * kept).astype(BF16)

    @pl.loop(0, NT // 2)
    def _(j):
        for a, queries in enumerate(unpacked(qg, j)):
            near_tile(a * (NT // 2) + j, queries)

    for d in range(1, Y):

        @pl.when(y >= d)
        def _():
            y_copy(d).wait_recv()

    def y_row(row):
        return ybuf[row, :QROWS].astype(F32)

    def y_end(row):
        return ybuf[row, QROWS:].astype(F32)[0:1, 0:1]

    @pl.when(y % 2 == 1)
    def _():
        ylow[:QROWS] = ybuf[y - 1, :QROWS]
        ymask[0] = jnp.broadcast_to(same(y_end(y - 1), first_doc), (8, HALF))

    @pl.when((y // 2) % 2 == 1)
    def _():
        base = (y // 4) * 4
        merged = y_row(base + 1) + same(y_end(base), y_end(base + 1)) * y_row(base)
        ylow[QROWS : 2 * QROWS] = merged.astype(BF16)
        ymask[1] = jnp.broadcast_to(same(y_end(base + 1), first_doc), (8, HALF))

    @pl.when(y >= 4)
    def _():
        early = y_row(1) + same(y_end(0), y_end(1)) * y_row(0)
        late = y_row(3) + same(y_end(2), y_end(3)) * y_row(2)
        merged = late + same(y_end(1), y_end(3)) * early
        ylow[2 * QROWS :] = merged.astype(BF16)
        ymask[2] = jnp.broadcast_to(same(y_end(3), first_doc), (8, HALF))

    b_copies = {}
    for d in (2, 1, 3):
        b_copies[d] = remote(ylow, yout.at[x], bs_sem.at[d], br_sem.at[d], at_x(d))
        b_copies[d].start()
    yout[x] = ylow[...]

    for d in (1, 3, 2):
        a_copies[d].wait_recv()
    before = xbuf[jnp.maximum(x - 1, 0), QROWS:].astype(F32)[0:1, 0:1]
    x_masks = [same(before, first_doc), same(ends[1], first_doc)]
    for b in range(2):
        rows = xout[:, b * QROWS : (b + 1) * QROWS, :].astype(F32).reshape(HALF, WIDTH)
        bucket[b * HALF : (b + 1) * HALF] = (rows * x_masks[b]).astype(BF16)

    @pl.loop(0, NT)
    def _(i):
        near[i] = near[i] + dot(qw[i, :, : 2 * HALF], bucket[: 2 * HALF])

    for d in (1, 3, 2):
        b_copies[d].wait_recv()
    for b in range(3):
        rows = yout[:, b * QROWS : (b + 1) * QROWS, :].astype(F32).reshape(HALF, WIDTH)
        mask = ymask[b][0:1, 0:1]
        bucket[(2 + b) * HALF : (3 + b) * HALF] = (rows * mask).astype(BF16)

    @pl.loop(0, NT)
    def _(i):
        total = near[i] + dot(qw[i, :, 2 * HALF :], bucket[2 * HALF :])
        out_ref[pl.ds(pl.multiple_of(i * TILE, TILE), TILE), :] = total.astype(BF16)

    for d in range(1, Z):
        k_copies[d].wait_send()
        q_copies[d].wait_send()
    for d in range(Z):
        k_partner(d).wait_send()
    q_partner.wait_send()
    for d in range(1, X):
        x_copies[d].wait_send()
        a_copies[d].wait_send()
        b_copies[d].wait_send()
    for d in range(1, Y):

        @pl.when(y + d < Y)
        def _():
            y_copy(d).wait_send()


def local(queries, key_vectors, values, level_table, level_class, doc_ids):
    tokens, width = values.shape
    vmem = pl.BlockSpec(memory_space=pltpu.VMEM)
    hbm = pl.BlockSpec(memory_space=pl.ANY)
    dma = pltpu.SemaphoreType.DMA
    return pl.pallas_call(
        body,
        out_shape=jax.ShapeDtypeStruct((tokens, width), BF16),
        in_specs=[hbm, hbm, hbm, vmem, vmem, vmem],
        out_specs=vmem,
        scratch_shapes=[
            pltpu.VMEM((8, tokens), BF16),
            pltpu.VMEM((8, tokens), BF16),
            pltpu.VMEM((tokens, width), BF16),
            pltpu.VMEM((2, Z, 16, tokens // 2), BF16),
            pltpu.VMEM((2, Z, 16, tokens // 2), BF16),
            pltpu.VMEM((NT, 32, TILE), BF16),
            pltpu.VMEM((32, 18 * HALF), BF16),
            pltpu.VMEM((NT, TILE, TILE), F32),
            pltpu.VMEM((NT, HALF, TILE), BF16),
            pltpu.VMEM((NT, HALF, WIDTH), F32),
            pltpu.VMEM((NT, HALF, WIDTH), BF16),
            pltpu.VMEM((4, HALF, WIDTH), BF16),
            pltpu.VMEM((HALF, WIDTH), BF16),
            pltpu.VMEM((X, TAGGED, WIDTH), BF16),
            pltpu.VMEM((X, TAGGED, WIDTH), BF16),
            pltpu.VMEM((X, 2 * QROWS, WIDTH), BF16),
            pltpu.VMEM((X, 2 * QROWS, WIDTH), BF16),
            pltpu.VMEM((TAGGED, WIDTH), BF16),
            pltpu.VMEM((Y, TAGGED, WIDTH), BF16),
            pltpu.VMEM((3 * QROWS, WIDTH), BF16),
            pltpu.VMEM((X, 3 * QROWS, WIDTH), BF16),
            pltpu.VMEM((3, 8, HALF), F32),
            pltpu.VMEM((FAR_LEVELS * HALF, WIDTH), BF16),
            pltpu.VMEM((NT, TILE, FAR_LEVELS * HALF), BF16),
            pltpu.VMEM((NT, TILE, WIDTH), F32),
            dma((3,)),
            dma((Z,)),
            dma((Z,)),
            dma((Z,)),
            dma((Z,)),
            dma((Z,)),
            dma((Z,)),
            dma((1,)),
            dma((1,)),
            dma((X,)),
            dma((X,)),
            dma((X,)),
            dma((X,)),
            dma((Y,)),
            dma((Y,)),
            dma((X,)),
            dma((X,)),
        ],
        compiler_params=pltpu.CompilerParams(
            collective_id=0, has_side_effects=True, vmem_limit_bytes=40 * 1024 * 1024
        ),
        name="block_and_levels",
    )(
        key_vectors.T,
        queries.T,
        values,
        level_table,
        level_class.reshape(tokens // HALF, HALF),
        doc_ids.reshape(tokens // HALF, HALF),
    )


def solution(mesh):
    in_specs = (P("seq", "head"), P("seq", "head"), P("seq", "head"), P(), P("seq"), P("seq"))
    out_specs = P("seq", "head")
    return jax.shard_map(local, mesh=mesh, in_specs=in_specs, out_specs=out_specs, check_vma=False)
```

```python
import jax
import jax.numpy as jnp
from jax import lax
from jax.experimental import pallas as pl
from jax.experimental.pallas import tpu as pltpu
from jax.sharding import PartitionSpec as P

MESH = pl.DeviceIdType.MESH
F32 = jnp.float32
BF16 = jnp.bfloat16

X = 4
Y = 8
Z = 8
TILE = 256
NT = 8
HALF = 128
WIDTH = 256
NEAR_LEVELS = 9
MID_LEVELS = 3
X_LEVELS = 2
Y_LEVELS = 3
FAR_LEVELS = X_LEVELS + Y_LEVELS
QROWS = 32
TAG = 16
TWO_HOPS = (2, 6, 1, 7)
FARTHEST_FIRST = (4, 3, 5, 2, 6, 1, 7)
DIM0 = (((0,), (0,)), ((), ()))


def dot(a, b):
    return jnp.dot(a, b, preferred_element_type=F32)


def same(a, b):
    return jnp.where(a == b, 1.0, 0.0).astype(F32)


def body(
    k_hbm,
    q_hbm,
    v_hbm,
    tab_hbm,
    cls_hbm,
    doc_hbm,
    near,
    qy,
    by,
    tab_ref,
    cls_ref,
    doc_ref,
    k8,
    q8,
    v,
    kg,
    qg,
    onehot,
    table,
    grid,
    kt,
    state,
    left9,
    left10,
    left11,
    tails,
    xtag,
    ytag,
    xbuf,
    xlow,
    xout,
    ysend,
    ybuf,
    ylow,
    yout,
    bx,
    qx,
    in_sem,
    ks_sem,
    kr_sem,
    kps_sem,
    kpr_sem,
    qs_sem,
    qr_sem,
    qps_sem,
    qpr_sem,
    xs_sem,
    xr_sem,
    as_sem,
    ar_sem,
    ys_sem,
    yr_sem,
    bs_sem,
    br_sem,
    ts_sem,
    tr_sem,
    us_sem,
    ur_sem,
    ready_sem,
):
    seq = lax.axis_index("seq")
    head = lax.axis_index("head")
    x = lax.rem(seq, X)
    y = lax.div(seq, X)
    z = lax.div(head, 2)
    c = lax.rem(head, 2)

    def at_z(d):
        return {"seq": seq, "head": lax.rem(z + d, Z) * 2 + c}

    def at_x(d):
        return {"seq": y * X + lax.rem(x + d, X), "head": head}

    def at_y(row):
        return {"seq": row * X + x, "head": head}

    partner = {"seq": seq, "head": z * 2 + (1 - c)}

    def remote(src, dst, send, recv, device):
        return pltpu.make_async_remote_copy(
            src_ref=src,
            dst_ref=dst,
            send_sem=send,
            recv_sem=recv,
            device_id=device,
            device_id_type=MESH,
        )

    load_k = pltpu.make_async_copy(k_hbm, k8, in_sem.at[0])
    load_q = pltpu.make_async_copy(q_hbm, q8, in_sem.at[1])
    load_v = pltpu.make_async_copy(v_hbm, v, in_sem.at[2])
    load_k.start()
    load_q.start()
    small_loads = [
        pltpu.make_async_copy(tab_hbm, tab_ref, in_sem.at[3]),
        pltpu.make_async_copy(cls_hbm, cls_ref, in_sem.at[4]),
        pltpu.make_async_copy(doc_hbm, doc_ref, in_sem.at[5]),
    ]
    for load in small_loads:
        load.start()
    load_v.start()

    barrier = pltpu.get_barrier_semaphore()
    peers = [at_z(d) for d in TWO_HOPS] + [at_x(d) for d in (2, 1, 3)]
    peers = peers + [at_y(lax.rem(y + d, Y)) for d in TWO_HOPS] + [partner]
    for peer in peers:
        pl.semaphore_signal(barrier, inc=1, device_id=peer, device_id_type=MESH)

    def pack(shard):
        wide = shard[...].astype(F32)
        return jnp.concatenate([wide[:, :1024], wide[:, 1024:]], axis=0).astype(BF16)

    load_k.wait()
    kg[c, z] = pack(k8)
    pl.semaphore_wait(barrier, len(peers))

    def gather(slots, send, recv):
        def own(d):
            return remote(slots.at[c, z], slots.at[c, z], send.at[d], recv.at[d], at_z(d))

        def onward(back, hop, index, part):
            slot = slots.at[c, lax.rem(z + Z - back, Z), :, part]
            return remote(slot, slot, send.at[index], recv.at[index], at_z(hop))

        steps = {d: own(d) for d in TWO_HOPS}
        steps[3] = onward(2, 1, 3, pl.ds(0, 1024))
        steps[5] = onward(6, 7, 5, pl.ds(0, 1024))
        steps[4] = onward(2, 2, 4, pl.ds(0, 512))
        steps[8] = onward(6, 6, 8, pl.ds(512, 512))
        return steps

    k_steps = gather(kg, ks_sem, kr_sem)
    q_steps = gather(qg, qs_sem, qr_sem)
    for d in TWO_HOPS:
        k_steps[d].start()

    def k_partner(d):
        slot = kg.at[c, lax.rem(z + Z - d, Z)]
        return remote(slot, slot, kps_sem.at[d], kpr_sem.at[d], partner)

    k_partner(0).start()
    for d in (2, 6):
        row = lax.rem(y + d, Y)
        pl.semaphore_signal(
            ready_sem.at[d // 4], inc=1, device_id=at_y(row), device_id_type=MESH
        )
    for load in small_loads:
        load.wait()
    load_q.wait()
    qg[c, z] = pack(q8)

    def last_doc(i):
        return doc_ref[2 * i + 1 : 2 * i + 2, HALF - 1 : HALF].astype(F32)

    xtag[x] = jnp.broadcast_to(last_doc(NT - 1), (TAG, HALF)).astype(BF16)
    t_copies = {}
    for d in (2, 1, 3):
        t_copies[d] = remote(xtag.at[x], xtag.at[x], ts_sem.at[d], tr_sem.at[d], at_x(d))
        t_copies[d].start()

    for order, level in enumerate(list(range(NEAR_LEVELS)) + [None] + list(range(NEAR_LEVELS, 17))):
        columns = slice(order * HALF, (order + 1) * HALF)
        if level is None:
            row = lax.broadcasted_iota(jnp.int32, (32, HALF), 0)
            table[:, columns] = jnp.where(row == 24, 1.0, 0.0).astype(BF16)
        else:
            weight = jnp.broadcast_to(tab_ref[:, level : level + 1], (8, HALF))
            high = weight.astype(BF16).astype(F32)
            middle = (weight - high).astype(BF16).astype(F32)
            low = weight - high - middle
            parts = [high, middle, low, jnp.zeros_like(low)]
            table[:, columns] = jnp.concatenate(parts, axis=0).astype(BF16)

    def doc_row(block):
        return doc_ref[pl.ds(block, 1), :].astype(F32)

    def doc_tile(i):
        return jnp.concatenate([doc_row(2 * i), doc_row(2 * i + 1)], axis=1)

    first_doc = doc_ref[0:1, 0:1].astype(F32)

    def grid_tile(i):
        row8 = lax.broadcasted_iota(jnp.int32, (8, TILE), 0)
        classes = jnp.concatenate(
            [cls_ref[pl.ds(2 * i, 1), :], cls_ref[pl.ds(2 * i + 1, 1), :]], axis=1
        )
        hot = jnp.where(row8 == classes, 1.0, 0.0).astype(F32)
        docs = jnp.where(row8 == 0, doc_tile(i), 0.0)
        onehot[i] = jnp.concatenate([hot, hot, hot, docs], axis=0).astype(BF16)
        wide = lax.dot_general(
            onehot[i], table[:, : 10 * HALF], DIM0, preferred_element_type=F32
        )
        t_pos = lax.broadcasted_iota(jnp.int32, (HALF, HALF), 0)
        s_pos = lax.broadcasted_iota(jnp.int32, (HALF, HALF), 1)
        apart = t_pos ^ s_pos
        causal = s_pos <= t_pos
        for a in range(2):
            rows = slice(a * HALF, (a + 1) * HALF)
            doc_t = wide[rows, 9 * HALF : 10 * HALF]
            weight = wide[rows, :HALF]
            for level in range(1, 8):
                column = wide[rows, level * HALF : (level + 1) * HALF]
                weight = jnp.where(apart >= 1 << (level - 1), column, weight)
            allowed = causal & (doc_t == doc_row(2 * i + a))
            grid[i, rows, rows] = jnp.where(allowed, weight, 0.0)
            if a == 1:
                weight = wide[rows, 8 * HALF : 9 * HALF]
                grid[i, rows, :HALF] = jnp.where(doc_t == doc_row(2 * i), weight, 0.0)
            else:
                grid[i, rows, HALF:] = jnp.zeros((HALF, HALF), F32)

    @pl.loop(0, NT // 2)
    def _(i):
        grid_tile(i)

    for d, first, second in ((2, 3, 4), (6, 5, 8)):
        k_steps[d].wait_recv()
        k_steps[first].start()
        k_steps[second].start()
    k_partner(2).start()
    k_partner(6).start()
    for d in (1, 7):
        k_steps[d].wait_recv()
        k_partner(d).start()

    for d in (1, 3, 2):
        t_copies[d].wait_recv()
    ytag[y] = xtag[X - 1]
    for side in range(2):
        pl.semaphore_wait(ready_sem.at[side], 1)

    def u_copy(d):
        row = lax.rem(y + d, Y)
        return remote(ytag.at[y], ytag.at[y], us_sem.at[d], ur_sem.at[d], at_y(row))

    for d in FARTHEST_FIRST:

        @pl.when(y + d < Y)
        def _():
            u_copy(d).start()

    @pl.loop(NT // 2, NT)
    def _(i):
        grid_tile(i)

    by[...] = jnp.zeros_like(by)
    load_v.wait()
    for d in (3, 5):
        k_steps[d].wait_recv()
        k_partner(d).start()
    k_steps[4].wait_recv()
    k_steps[8].wait_recv()
    k_partner(4).start()
    for d in TWO_HOPS:
        q_steps[d].start()
    for d in (0, 2, 6, 1, 7, 3, 5, 4):
        k_partner(d).wait_recv()

    def unpacked(gathered, j):
        wide = gathered[:, :, :, pl.ds(pl.multiple_of(j * TILE, TILE), TILE)].astype(F32)
        return [wide[:, :, 8 * a : 8 * a + 8, :].reshape(HALF, TILE) for a in range(2)]

    @pl.loop(0, NT // 2)
    def _(j):
        for a, keys in enumerate(unpacked(kg, j)):
            i = a * (NT // 2) + j
            docs = doc_tile(i)
            kept = jnp.where(docs == docs[:, TILE - 1 : TILE], keys, 0.0)
            kt[i] = keys.astype(BF16)
            part = dot(kept.astype(BF16), v[pl.ds(pl.multiple_of(i * TILE, TILE), TILE), :])
            state[i] = part
            left9[i] = part.astype(BF16)

    level_states = [state[i] for i in range(NT)]
    pairs = [
        level_states[2 * j + 1] + same(last_doc(2 * j), last_doc(2 * j + 1)) * level_states[2 * j]
        for j in range(4)
    ]
    for j in range(4):
        left10[j] = pairs[j].astype(BF16)
    quads = [
        pairs[2 * j + 1] + same(last_doc(4 * j + 1), last_doc(4 * j + 3)) * pairs[2 * j]
        for j in range(2)
    ]
    left11[...] = quads[0].astype(BF16)
    tail = quads[1] + same(last_doc(3), last_doc(7)) * quads[0]
    for p in range(X):
        tails[p] = tail[p * QROWS : (p + 1) * QROWS].astype(BF16)

    x_copies = {}
    for d in (2, 1, 3):
        x_copies[d] = remote(
            tails.at[lax.rem(x + d, X)], xbuf.at[x], xs_sem.at[d], xr_sem.at[d], at_x(d)
        )
        x_copies[d].start()
    xbuf[x] = tails[x]

    for d, first, second in ((2, 3, 4), (6, 5, 8)):
        q_steps[d].wait_recv()
        q_steps[first].start()
        q_steps[second].start()

    for d in (1, 3, 2):
        x_copies[d].wait_recv()
    ends = [xtag[p].astype(F32)[0:1, 0:1] for p in range(X)]
    terms = [xbuf[p].astype(F32) for p in range(X)]
    low_pair = terms[1] + same(ends[0], ends[1]) * terms[0]
    high_pair = terms[3] + same(ends[2], ends[3]) * terms[2]
    row_tail = high_pair + same(ends[1], ends[3]) * low_pair
    ysend[...] = row_tail.astype(BF16)

    def y_copy(d):
        row = lax.rem(y + d, Y)
        return remote(ysend, ybuf.at[y], ys_sem.at[d], yr_sem.at[d], at_y(row))

    for d in FARTHEST_FIRST:

        @pl.when(y + d < Y)
        def _():
            y_copy(d).start()

    blank = jnp.zeros((QROWS, WIDTH), BF16)
    xlow[0, :QROWS] = blank
    xlow[0, QROWS:] = blank
    xlow[1, :QROWS] = xbuf[0]
    xlow[1, QROWS:] = blank
    xlow[2, :QROWS] = blank
    xlow[2, QROWS:] = low_pair.astype(BF16)
    xlow[3, :QROWS] = xbuf[2]
    xlow[3, QROWS:] = low_pair.astype(BF16)
    a_copies = {}
    for d in (2, 1, 3):
        a_copies[d] = remote(
            xlow.at[lax.rem(x + d, X)], xout.at[x], as_sem.at[d], ar_sem.at[d], at_x(d)
        )
        a_copies[d].start()
    xout[x] = xlow[x]

    for d in (1, 7, 3, 5, 4, 8):
        q_steps[d].wait_recv()
    q_partner = remote(qg.at[c], qg.at[c], qps_sem.at[0], qpr_sem.at[0], partner)
    q_partner.start()
    q_partner.wait_recv()

    def near_tile(i, queries):
        turned = queries.T
        rows = pl.ds(pl.multiple_of(i * TILE, TILE), TILE)
        scores = dot(turned.astype(BF16), kt[i])
        weighted = (scores * grid[i]).astype(BF16)
        total = dot(weighted, v[rows, :])
        wide = lax.dot_general(
            onehot[i], table[:, 9 * HALF :], DIM0, preferred_element_type=F32
        )
        doc_t = wide[:, :HALF]
        mids = []
        for b in range(MID_LEVELS):
            end = jnp.maximum((i >> b << b) - 1, 0)
            end_doc = doc_row(2 * end + 1)[:, HALF - 1 : HALF]
            present = jnp.where((i >> b) % 2 == 1, 1.0, 0.0).astype(F32)
            weight = jnp.where(doc_t == end_doc, wide[:, (1 + b) * HALF : (2 + b) * HALF], 0.0)
            mids.append((weight * (turned * present)).astype(BF16))
        lefts = [
            left9[jnp.maximum(i - 1, 0)],
            left10[jnp.maximum((i >> 1) - 1, 0)],
            left11[...],
        ]
        total = total + dot(jnp.concatenate(mids, axis=1), jnp.concatenate(lefts, axis=0))
        near[i] = total
        kept = jnp.where(doc_t == first_doc, turned, 0.0)
        for b in range(FAR_LEVELS):
            start = (1 + MID_LEVELS + b) * HALF
            target, place = (qx, b) if b < X_LEVELS else (qy, b - X_LEVELS)
            columns = slice(place * HALF, (place + 1) * HALF)
            target[i, :, columns] = (wide[:, start : start + HALF] * kept).astype(BF16)

    @pl.loop(0, NT // 4)
    def _(j):
        for a, queries in enumerate(unpacked(qg, j)):
            near_tile(a * (NT // 2) + j, queries)

    for d in range(1, Y):

        @pl.when(y >= d)
        def _():
            u_copy(d).wait_recv()

    def y_row(row):
        return ybuf[row].astype(F32)

    def y_end(row):
        return ytag[row].astype(F32)[0:1, 0:1]

    def b_copy(b, d):
        index = b * X + d
        return remote(ylow.at[b], yout.at[x, b], bs_sem.at[index], br_sem.at[index], at_x(d))

    def hand_on(b, merged):
        ylow[b] = merged
        yout[x, b] = merged
        for d in (2, 1, 3):
            b_copy(b, d).start()

    bits = [lax.rem(y, 2) == 1, lax.rem(lax.div(y, 2), 2) == 1, y >= 4]
    four = lax.div(y, 4) * 4

    @pl.when(bits[0])
    def _():
        y_copy(1).wait_recv()
        hand_on(0, ybuf[y - 1])

    @pl.when(bits[1])
    def _():
        for d in range(2):
            y_copy(y - four - d).wait_recv()
        merged = y_row(four + 1) + same(y_end(four), y_end(four + 1)) * y_row(four)
        hand_on(1, merged.astype(BF16))

    @pl.when(bits[2])
    def _():
        for d in range(4):
            y_copy(y - d).wait_recv()
        early = y_row(1) + same(y_end(0), y_end(1)) * y_row(0)
        late = y_row(3) + same(y_end(2), y_end(3)) * y_row(2)
        merged = late + same(y_end(1), y_end(3)) * early
        hand_on(2, merged.astype(BF16))

    @pl.loop(NT // 4, NT // 2)
    def _(j):
        for a, queries in enumerate(unpacked(qg, j)):
            near_tile(a * (NT // 2) + j, queries)

    for d in (1, 3, 2):
        a_copies[d].wait_recv()
    before = xtag[jnp.maximum(x - 1, 0)].astype(F32)[0:1, 0:1]
    x_masks = [same(before, first_doc), same(ends[1], first_doc)]
    for b in range(2):
        rows = xout[:, b * QROWS : (b + 1) * QROWS, :].astype(F32).reshape(HALF, WIDTH)
        bx[b * HALF : (b + 1) * HALF] = (rows * x_masks[b]).astype(BF16)

    @pl.loop(0, NT // 2)
    def _(j):
        for i in (2 * j, 2 * j + 1):
            near[i] = near[i] + dot(qx[i], bx[...])

    y_ends = [y - 1, four + 1, 3]
    for b in range(Y_LEVELS):

        @pl.when(bits[b])
        def _():
            for d in (1, 3, 2):
                b_copy(b, d).wait_recv()
            rows = yout[:, b].astype(F32).reshape(HALF, WIDTH)
            mask = same(y_end(y_ends[b]), first_doc)
            by[b * HALF : (b + 1) * HALF] = (rows * mask).astype(BF16)

    for step in k_steps:
        k_steps[step].wait_send()
        q_steps[step].wait_send()
    for d in range(Z):
        k_partner(d).wait_send()
    q_partner.wait_send()
    for d in range(1, X):
        t_copies[d].wait_send()
        x_copies[d].wait_send()
        a_copies[d].wait_send()
    for b in range(Y_LEVELS):

        @pl.when(bits[b])
        def _():
            for d in range(1, X):
                b_copy(b, d).wait_send()

    for d in range(1, Y):

        @pl.when(y + d < Y)
        def _():
            u_copy(d).wait_send()
            y_copy(d).wait_send()


def last(near, qy, by, out_hbm, out, out_sem):
    copies = []
    for i in range(NT):
        rows = pl.ds(i * TILE, TILE)
        out[rows, :] = (near[i] + dot(qy[i], by[...])).astype(BF16)
        copies.append(pltpu.make_async_copy(out.at[rows], out_hbm.at[rows], out_sem.at[i]))
        copies[i].start()
    for copy in copies:
        copy.wait()


def local(queries, key_vectors, values, level_table, level_class, doc_ids):
    tokens, width = values.shape
    vmem = pl.BlockSpec(memory_space=pltpu.VMEM)
    hbm = pl.BlockSpec(memory_space=pltpu.HBM)
    dma = pltpu.SemaphoreType.DMA
    arguments = (
        key_vectors.T,
        queries.T,
        values,
        level_table,
        level_class.reshape(tokens // HALF, HALF),
        doc_ids.reshape(tokens // HALF, HALF),
    )
    near, qy, by = pl.pallas_call(
        body,
        out_shape=[
            pltpu.VMEM((NT, TILE, WIDTH), F32),
            pltpu.VMEM((NT, TILE, Y_LEVELS * HALF), BF16),
            pltpu.VMEM((Y_LEVELS * HALF, WIDTH), BF16),
        ],
        in_specs=[hbm] * 6,
        out_specs=[vmem] * 3,
        scratch_shapes=[
            pltpu.VMEM(level_table.shape, F32),
            pltpu.VMEM((tokens // HALF, HALF), jnp.int32),
            pltpu.VMEM((tokens // HALF, HALF), jnp.int32),
            pltpu.VMEM((8, tokens), BF16),
            pltpu.VMEM((8, tokens), BF16),
            pltpu.VMEM((tokens, width), BF16),
            pltpu.VMEM((2, Z, 16, tokens // 2), BF16),
            pltpu.VMEM((2, Z, 16, tokens // 2), BF16),
            pltpu.VMEM((NT, 32, TILE), BF16),
            pltpu.VMEM((32, 18 * HALF), BF16),
            pltpu.VMEM((NT, TILE, TILE), F32),
            pltpu.VMEM((NT, HALF, TILE), BF16),
            pltpu.VMEM((NT, HALF, WIDTH), F32),
            pltpu.VMEM((NT, HALF, WIDTH), BF16),
            pltpu.VMEM((4, HALF, WIDTH), BF16),
            pltpu.VMEM((HALF, WIDTH), BF16),
            pltpu.VMEM((X, QROWS, WIDTH), BF16),
            pltpu.VMEM((X, TAG, HALF), BF16),
            pltpu.VMEM((Y, TAG, HALF), BF16),
            pltpu.VMEM((X, QROWS, WIDTH), BF16),
            pltpu.VMEM((X, 2 * QROWS, WIDTH), BF16),
            pltpu.VMEM((X, 2 * QROWS, WIDTH), BF16),
            pltpu.VMEM((QROWS, WIDTH), BF16),
            pltpu.VMEM((Y, QROWS, WIDTH), BF16),
            pltpu.VMEM((Y_LEVELS, QROWS, WIDTH), BF16),
            pltpu.VMEM((X, Y_LEVELS, QROWS, WIDTH), BF16),
            pltpu.VMEM((X_LEVELS * HALF, WIDTH), BF16),
            pltpu.VMEM((NT, TILE, X_LEVELS * HALF), BF16),
            dma((6,)),
            dma((Z + 1,)),
            dma((Z + 1,)),
            dma((Z,)),
            dma((Z,)),
            dma((Z + 1,)),
            dma((Z + 1,)),
            dma((1,)),
            dma((1,)),
            dma((X,)),
            dma((X,)),
            dma((X,)),
            dma((X,)),
            dma((Y,)),
            dma((Y,)),
            dma((Y_LEVELS * X,)),
            dma((Y_LEVELS * X,)),
            dma((X,)),
            dma((X,)),
            dma((Y,)),
            dma((Y,)),
            pltpu.SemaphoreType.REGULAR((2,)),
        ],
        compiler_params=pltpu.CompilerParams(
            collective_id=0, has_side_effects=True, vmem_limit_bytes=40 * 1024 * 1024
        ),
        name="blocks_and_states",
    )(*[pltpu.with_memory_space_constraint(a, pltpu.HBM) for a in arguments])
    return pl.pallas_call(
        last,
        out_shape=jax.ShapeDtypeStruct((tokens, width), BF16),
        in_specs=[vmem] * 3,
        out_specs=pl.BlockSpec(memory_space=pltpu.HBM),
        scratch_shapes=[pltpu.VMEM((tokens, width), BF16), dma((NT,))],
        compiler_params=pltpu.CompilerParams(vmem_limit_bytes=16 * 1024 * 1024),
        name="rows_before",
    )(near, qy, by)


def solution(mesh):
    in_specs = (P("seq", "head"), P("seq", "head"), P("seq", "head"), P(), P("seq"), P("seq"))
    out_specs = P("seq", "head")
    return jax.shard_map(local, mesh=mesh, in_specs=in_specs, out_specs=out_specs, check_vma=False)
```

```python
import jax
import jax.numpy as jnp
from jax import lax
from jax.experimental import pallas as pl
from jax.experimental.pallas import tpu as pltpu
from jax.sharding import PartitionSpec as P

MESH = pl.DeviceIdType.MESH
F32 = jnp.float32
BF16 = jnp.bfloat16

X = 4
Y = 8
Z = 8
TILE = 256
NT = 8
HALF = 128
WIDTH = 256
NEAR_LEVELS = 9
MID_LEVELS = 3
X_LEVELS = 2
Y_LEVELS = 3
FAR_LEVELS = X_LEVELS + Y_LEVELS
LANE = 64
QROWS = 16
TAG = 16
TWO_HOPS = (2, 6, 1, 7)
FARTHEST_FIRST = (4, 3, 5, 2, 6, 1, 7)
DIM0 = (((0,), (0,)), ((), ()))


def dot(a, b):
    return jnp.dot(a, b, preferred_element_type=F32)


def same(a, b):
    return jnp.where(a == b, 1.0, 0.0).astype(F32)


def body(
    k_hbm,
    q_hbm,
    v_hbm,
    tab_hbm,
    cls_hbm,
    doc_hbm,
    near,
    qy,
    by,
    tab_ref,
    cls_ref,
    doc_ref,
    v,
    v_beside,
    kg,
    qg,
    onehot,
    table,
    grid,
    kt,
    state,
    left9,
    left10,
    left11,
    tails,
    xtag,
    ytag,
    xbuf,
    xlow,
    xout,
    ysend,
    ybuf,
    ylow,
    yout,
    bx,
    qx,
    in_sem,
    ks_sem,
    kr_sem,
    kps_sem,
    kpr_sem,
    qs_sem,
    qr_sem,
    qps_sem,
    qpr_sem,
    xs_sem,
    xr_sem,
    as_sem,
    ar_sem,
    ys_sem,
    yr_sem,
    bs_sem,
    br_sem,
    ts_sem,
    tr_sem,
    us_sem,
    ur_sem,
    ready_sem,
    vs_sem,
    vr_sem,
):
    seq = lax.axis_index("seq")
    head = lax.axis_index("head")
    x = lax.rem(seq, X)
    y = lax.div(seq, X)
    z = lax.div(head, 2)
    c = lax.rem(head, 2)

    def at_z(d):
        return {"seq": seq, "head": lax.rem(z + d, Z) * 2 + c}

    def at_x(d):
        return {"seq": y * X + lax.rem(x + d, X), "head": head}

    def beside_x(d):
        return {"seq": y * X + lax.rem(x + d, X), "head": z * 2 + (1 - c)}

    def at_y(row):
        return {"seq": row * X + x, "head": head}

    partner = {"seq": seq, "head": z * 2 + (1 - c)}

    def remote(src, dst, send, recv, device):
        return pltpu.make_async_remote_copy(
            src_ref=src,
            dst_ref=dst,
            send_sem=send,
            recv_sem=recv,
            device_id=device,
            device_id_type=MESH,
        )

    barrier = pltpu.get_barrier_semaphore()
    peers = [at_z(d) for d in TWO_HOPS] + [at_x(d) for d in (2, 1, 3)]
    peers = peers + [at_y(lax.rem(y + d, Y)) for d in TWO_HOPS]
    peers = peers + [beside_x(d) for d in (2, 1, 3, 0)]
    for peer in peers:
        pl.semaphore_signal(barrier, inc=1, device_id=peer, device_id_type=MESH)

    load_k = pltpu.make_async_copy(k_hbm, kg.at[c, z], in_sem.at[0])
    load_q = pltpu.make_async_copy(q_hbm, qg.at[c, z], in_sem.at[1])
    load_v = pltpu.make_async_copy(v_hbm, v, in_sem.at[2])
    load_k.start()
    load_q.start()
    small_loads = [
        pltpu.make_async_copy(tab_hbm, tab_ref, in_sem.at[3]),
        pltpu.make_async_copy(cls_hbm, cls_ref, in_sem.at[4]),
        pltpu.make_async_copy(doc_hbm, doc_ref, in_sem.at[5]),
    ]
    for load in small_loads:
        load.start()
    load_v.start()

    pl.semaphore_wait(barrier, len(peers))

    def gather(shard, slots, send, recv):
        def own(d):
            return remote(shard, slots.at[c, z], send.at[d], recv.at[d], at_z(d))

        def onward(back, hop, index, part):
            slot = slots.at[c, lax.rem(z + Z - back, Z), :, part]
            return remote(slot, slot, send.at[index], recv.at[index], at_z(hop))

        steps = {d: own(d) for d in TWO_HOPS}
        steps[3] = onward(2, 1, 3, pl.ds(0, 1024))
        steps[5] = onward(6, 7, 5, pl.ds(0, 1024))
        steps[4] = onward(2, 2, 4, pl.ds(0, 512))
        steps[8] = onward(6, 6, 8, pl.ds(512, 512))
        return steps

    k_steps = gather(k_hbm, kg, ks_sem, kr_sem)
    q_steps = gather(q_hbm, qg, qs_sem, qr_sem)
    for d in TWO_HOPS:
        k_steps[d].start()

    def k_partner(d):
        slot = kg.at[c, lax.rem(z + Z - d, Z)]
        return remote(slot, slot, kps_sem.at[d], kpr_sem.at[d], partner)

    v_across = remote(v_hbm, v_beside, vs_sem.at[0], vr_sem.at[0], partner)
    v_across.start()
    load_k.wait()
    k_partner(0).start()
    for d in (2, 6):
        row = lax.rem(y + d, Y)
        pl.semaphore_signal(
            ready_sem.at[d // 4], inc=1, device_id=at_y(row), device_id_type=MESH
        )
    for load in small_loads:
        load.wait()
    load_q.wait()

    def last_doc(i):
        return doc_ref[2 * i + 1 : 2 * i + 2, HALF - 1 : HALF].astype(F32)

    xtag[x] = jnp.broadcast_to(last_doc(NT - 1), (TAG, HALF)).astype(BF16)
    t_copies = {}
    for d in (2, 1, 3):
        t_copies[d] = remote(xtag.at[x], xtag.at[x], ts_sem.at[d], tr_sem.at[d], at_x(d))
        t_copies[d].start()

    for order, level in enumerate(list(range(NEAR_LEVELS)) + [None] + list(range(NEAR_LEVELS, 17))):
        columns = slice(order * HALF, (order + 1) * HALF)
        if level is None:
            row = lax.broadcasted_iota(jnp.int32, (32, HALF), 0)
            table[:, columns] = jnp.where(row == 24, 1.0, 0.0).astype(BF16)
        else:
            weight = jnp.broadcast_to(tab_ref[:, level : level + 1], (8, HALF))
            high = weight.astype(BF16).astype(F32)
            middle = (weight - high).astype(BF16).astype(F32)
            low = weight - high - middle
            parts = [high, middle, low, jnp.zeros_like(low)]
            table[:, columns] = jnp.concatenate(parts, axis=0).astype(BF16)

    def doc_row(block):
        return doc_ref[pl.ds(block, 1), :].astype(F32)

    def doc_tile(i):
        return jnp.concatenate([doc_row(2 * i), doc_row(2 * i + 1)], axis=1)

    first_doc = doc_ref[0:1, 0:1].astype(F32)

    def grid_tile(i):
        row8 = lax.broadcasted_iota(jnp.int32, (8, TILE), 0)
        classes = jnp.concatenate(
            [cls_ref[pl.ds(2 * i, 1), :], cls_ref[pl.ds(2 * i + 1, 1), :]], axis=1
        )
        hot = jnp.where(row8 == classes, 1.0, 0.0).astype(F32)
        docs = jnp.where(row8 == 0, doc_tile(i), 0.0)
        onehot[i] = jnp.concatenate([hot, hot, hot, docs], axis=0).astype(BF16)
        wide = lax.dot_general(
            onehot[i], table[:, : 10 * HALF], DIM0, preferred_element_type=F32
        )
        t_pos = lax.broadcasted_iota(jnp.int32, (HALF, HALF), 0)
        s_pos = lax.broadcasted_iota(jnp.int32, (HALF, HALF), 1)
        apart = t_pos ^ s_pos
        causal = s_pos <= t_pos
        for a in range(2):
            rows = slice(a * HALF, (a + 1) * HALF)
            doc_t = wide[rows, 9 * HALF : 10 * HALF]
            weight = wide[rows, :HALF]
            for level in range(1, 8):
                column = wide[rows, level * HALF : (level + 1) * HALF]
                weight = jnp.where(apart >= 1 << (level - 1), column, weight)
            allowed = causal & (doc_t == doc_row(2 * i + a))
            grid[i, rows, rows] = jnp.where(allowed, weight, 0.0)
            if a == 1:
                weight = wide[rows, 8 * HALF : 9 * HALF]
                grid[i, rows, :HALF] = jnp.where(doc_t == doc_row(2 * i), weight, 0.0)
            else:
                grid[i, rows, HALF:] = jnp.zeros((HALF, HALF), F32)

    @pl.loop(0, NT // 2)
    def _(i):
        grid_tile(i)

    for d, first, second in ((2, 3, 4), (6, 5, 8)):
        k_steps[d].wait_recv()
        k_steps[first].start()
        k_steps[second].start()
    k_partner(2).start()
    k_partner(6).start()
    for d in (1, 7):
        k_steps[d].wait_recv()
        k_partner(d).start()

    for d in TWO_HOPS:
        q_steps[d].start()
    for d in (1, 3, 2):
        t_copies[d].wait_recv()
    ytag[y] = xtag[X - 1]
    for side in range(2):
        pl.semaphore_wait(ready_sem.at[side], 1)

    def u_copy(d):
        row = lax.rem(y + d, Y)
        return remote(ytag.at[y], ytag.at[y], us_sem.at[d], ur_sem.at[d], at_y(row))

    for d in FARTHEST_FIRST:

        @pl.when(y + d < Y)
        def _():
            u_copy(d).start()

    @pl.loop(NT // 2, NT)
    def _(i):
        grid_tile(i)

    by[...] = jnp.zeros_like(by)
    load_v.wait()
    for d in (3, 5):
        k_steps[d].wait_recv()
        k_partner(d).start()
    k_steps[4].wait_recv()
    k_steps[8].wait_recv()
    k_partner(4).start()
    v_across.wait_recv()
    end_doc = last_doc(NT - 1)
    mine = jnp.zeros((LANE, WIDTH), F32)
    theirs = jnp.zeros((LANE, WIDTH), F32)
    for a in range(2):
        keys = kg[c].astype(F32)[:, 8 * a : 8 * a + 8, :]
        docs = jnp.concatenate([doc_row(8 * a + i) for i in range(8)], axis=1)
        kept = jnp.where(docs == end_doc, keys.reshape(LANE, 1024), 0.0).astype(BF16)
        mine = mine + dot(kept, v[a * 1024 : (a + 1) * 1024, :])
        theirs = theirs + dot(kept, v_beside[a * 1024 : (a + 1) * 1024, :])
    for p in range(X):
        tails[p, c] = mine[p * QROWS : (p + 1) * QROWS].astype(BF16)
        tails[p, 1 - c] = theirs[p * QROWS : (p + 1) * QROWS].astype(BF16)

    x_copies = {}
    for d in (2, 1, 3):
        x_copies[d] = remote(
            tails.at[lax.rem(x + d, X)], xbuf.at[x], xs_sem.at[d], xr_sem.at[d], at_x(d)
        )
        x_copies[d].start()
    xbuf[x] = tails[x]
    for d, first, second in ((2, 3, 4), (6, 5, 8)):
        q_steps[d].wait_recv()
        q_steps[first].start()
        q_steps[second].start()

    for d in (0, 2, 6, 1, 7, 3, 5, 4):
        k_partner(d).wait_recv()

    def unpacked(gathered, j):
        wide = gathered[:, :, :, pl.ds(pl.multiple_of(j * TILE, TILE), TILE)].astype(F32)
        return [wide[:, :, 8 * a : 8 * a + 8, :].reshape(HALF, TILE) for a in range(2)]

    @pl.loop(0, NT // 2)
    def _(j):
        for a, keys in enumerate(unpacked(kg, j)):
            i = a * (NT // 2) + j
            docs = doc_tile(i)
            kept = jnp.where(docs == docs[:, TILE - 1 : TILE], keys, 0.0)
            kt[i] = keys.astype(BF16)
            part = dot(kept.astype(BF16), v[pl.ds(pl.multiple_of(i * TILE, TILE), TILE), :])
            state[i] = part
            left9[i] = part.astype(BF16)

    level_states = [state[i] for i in range(NT)]
    pairs = [
        level_states[2 * j + 1] + same(last_doc(2 * j), last_doc(2 * j + 1)) * level_states[2 * j]
        for j in range(4)
    ]
    for j in range(4):
        left10[j] = pairs[j].astype(BF16)
    first_quad = pairs[1] + same(last_doc(1), last_doc(3)) * pairs[0]
    left11[...] = first_quad.astype(BF16)

    for d in (1, 3, 2):
        x_copies[d].wait_recv()
    ends = [xtag[p].astype(F32)[0:1, 0:1] for p in range(X)]
    terms = [xbuf[p].astype(F32) for p in range(X)]
    low_pair = terms[1] + same(ends[0], ends[1]) * terms[0]
    high_pair = terms[3] + same(ends[2], ends[3]) * terms[2]
    row_tail = high_pair + same(ends[1], ends[3]) * low_pair
    ysend[...] = row_tail.astype(BF16)

    def y_copy(d):
        row = lax.rem(y + d, Y)
        return remote(ysend, ybuf.at[y], ys_sem.at[d], yr_sem.at[d], at_y(row))

    for d in FARTHEST_FIRST:

        @pl.when(y + d < Y)
        def _():
            y_copy(d).start()

    blank = jnp.zeros((2, QROWS, WIDTH), BF16)
    low = low_pair.astype(BF16)
    pieces = [(blank, blank), (xbuf[0], blank), (blank, low), (xbuf[2], low)]
    for p in range(X):
        for b in range(X_LEVELS):
            for core in range(2):
                xlow[p, core, b] = pieces[p][b][core]

    def fan_out(make):
        return [make(d, d, at_x(d), c) for d in (2, 1, 3)] + [
            make(d, X + d, beside_x(d), 1 - c) for d in (2, 1, 3, 0)
        ]

    def a_copy(d, index, device, core):
        source = xlow.at[lax.rem(x + d, X), core]
        return remote(source, xout.at[c, x], as_sem.at[index], ar_sem.at[index], device)

    a_copies = fan_out(a_copy)
    for copy in a_copies:
        copy.start()
    xout[c, x] = xlow[x, c]

    for d in (1, 7, 3, 5, 4, 8):
        q_steps[d].wait_recv()
    q_partner = remote(qg.at[c], qg.at[c], qps_sem.at[0], qpr_sem.at[0], partner)
    q_partner.start()

    q_partner.wait_recv()

    def near_tile(i, queries):
        turned = queries.T
        rows = pl.ds(pl.multiple_of(i * TILE, TILE), TILE)
        scores = dot(turned.astype(BF16), kt[i])
        weighted = (scores * grid[i]).astype(BF16)
        total = dot(weighted, v[rows, :])
        wide = lax.dot_general(
            onehot[i], table[:, 9 * HALF :], DIM0, preferred_element_type=F32
        )
        doc_t = wide[:, :HALF]
        mids = []
        for b in range(MID_LEVELS):
            end = jnp.maximum((i >> b << b) - 1, 0)
            end_doc = doc_row(2 * end + 1)[:, HALF - 1 : HALF]
            present = jnp.where((i >> b) % 2 == 1, 1.0, 0.0).astype(F32)
            weight = jnp.where(doc_t == end_doc, wide[:, (1 + b) * HALF : (2 + b) * HALF], 0.0)
            mids.append((weight * (turned * present)).astype(BF16))
        lefts = [
            left9[jnp.maximum(i - 1, 0)],
            left10[jnp.maximum((i >> 1) - 1, 0)],
            left11[...],
        ]
        total = total + dot(jnp.concatenate(mids, axis=1), jnp.concatenate(lefts, axis=0))
        near[i] = total
        kept = jnp.where(doc_t == first_doc, turned, 0.0)
        for b in range(FAR_LEVELS):
            start = (1 + MID_LEVELS + b) * HALF
            target, place = (qx, b) if b < X_LEVELS else (qy, b - X_LEVELS)
            columns = slice(place * HALF, (place + 1) * HALF)
            target[i, :, columns] = (wide[:, start : start + HALF] * kept).astype(BF16)

    @pl.loop(0, NT // 4)
    def _(j):
        for a, queries in enumerate(unpacked(qg, j)):
            near_tile(a * (NT // 2) + j, queries)

    for d in range(1, Y):

        @pl.when(y >= d)
        def _():
            u_copy(d).wait_recv()

    def y_row(row):
        return ybuf[row].astype(F32)

    def y_end(row):
        return ytag[row].astype(F32)[0:1, 0:1]

    def b_copies(b):
        def b_copy(d, index, device, core):
            send, recv = bs_sem.at[b * 2 * X + index], br_sem.at[b * 2 * X + index]
            return remote(ylow.at[b, core], yout.at[c, x, b], send, recv, device)

        return fan_out(b_copy)

    def hand_on(b, merged):
        ylow[b] = merged
        for copy in b_copies(b):
            copy.start()
        yout[c, x, b] = ylow[b, c]

    bits = [lax.rem(y, 2) == 1, lax.rem(lax.div(y, 2), 2) == 1, y >= 4]
    four = lax.div(y, 4) * 4

    @pl.when(bits[0])
    def _():
        y_copy(1).wait_recv()
        hand_on(0, ybuf[y - 1])

    @pl.when(bits[1])
    def _():
        for d in range(2):
            y_copy(y - four - d).wait_recv()
        merged = y_row(four + 1) + same(y_end(four), y_end(four + 1)) * y_row(four)
        hand_on(1, merged.astype(BF16))

    @pl.when(bits[2])
    def _():
        for d in range(4):
            y_copy(y - d).wait_recv()
        early = y_row(1) + same(y_end(0), y_end(1)) * y_row(0)
        late = y_row(3) + same(y_end(2), y_end(3)) * y_row(2)
        merged = late + same(y_end(1), y_end(3)) * early
        hand_on(2, merged.astype(BF16))

    @pl.loop(NT // 4, NT // 2)
    def _(j):
        for a, queries in enumerate(unpacked(qg, j)):
            near_tile(a * (NT // 2) + j, queries)

    for copy in a_copies:
        copy.wait_recv()
    before = xtag[jnp.maximum(x - 1, 0)].astype(F32)[0:1, 0:1]
    x_masks = [same(before, first_doc), same(ends[1], first_doc)]
    for b in range(2):
        rows = xout[:, :, b].astype(F32).reshape(HALF, WIDTH)
        bx[b * HALF : (b + 1) * HALF] = (rows * x_masks[b]).astype(BF16)

    @pl.loop(0, NT // 2)
    def _(j):
        for i in (2 * j, 2 * j + 1):
            near[i] = near[i] + dot(qx[i], bx[...])

    y_ends = [y - 1, four + 1, 3]
    for b in range(Y_LEVELS):

        @pl.when(bits[b])
        def _():
            for copy in b_copies(b):
                copy.wait_recv()
            rows = yout[:, :, b].astype(F32).reshape(HALF, WIDTH)
            mask = same(y_end(y_ends[b]), first_doc)
            by[b * HALF : (b + 1) * HALF] = (rows * mask).astype(BF16)

    for step in k_steps:
        k_steps[step].wait_send()
        q_steps[step].wait_send()
    for d in range(Z):
        k_partner(d).wait_send()
    q_partner.wait_send()
    v_across.wait_send()
    for d in range(1, X):
        t_copies[d].wait_send()
        x_copies[d].wait_send()
    for copy in a_copies:
        copy.wait_send()
    for b in range(Y_LEVELS):

        @pl.when(bits[b])
        def _():
            for copy in b_copies(b):
                copy.wait_send()

    for d in range(1, Y):

        @pl.when(y + d < Y)
        def _():
            u_copy(d).wait_send()
            y_copy(d).wait_send()


def last(near, qy, by, out_hbm, out, out_sem):
    copies = []
    for i in range(NT):
        rows = pl.ds(i * TILE, TILE)
        out[rows, :] = (near[i] + dot(qy[i], by[...])).astype(BF16)
        copies.append(pltpu.make_async_copy(out.at[rows], out_hbm.at[rows], out_sem.at[i]))
        copies[i].start()
    for copy in copies:
        copy.wait()


def folded(shard):
    tokens, width = shard.shape
    return shard.T.reshape(width, 2, tokens // 2).swapaxes(0, 1).reshape(2 * width, tokens // 2)


def local(queries, key_vectors, values, level_table, level_class, doc_ids):
    tokens, width = values.shape
    vmem = pl.BlockSpec(memory_space=pltpu.VMEM)
    hbm = pl.BlockSpec(memory_space=pltpu.HBM)
    dma = pltpu.SemaphoreType.DMA
    arguments = (
        folded(key_vectors),
        folded(queries),
        values,
        level_table,
        level_class.reshape(tokens // HALF, HALF),
        doc_ids.reshape(tokens // HALF, HALF),
    )
    near, qy, by = pl.pallas_call(
        body,
        out_shape=[
            pltpu.VMEM((NT, TILE, WIDTH), F32),
            pltpu.VMEM((NT, TILE, Y_LEVELS * HALF), BF16),
            pltpu.VMEM((Y_LEVELS * HALF, WIDTH), BF16),
        ],
        in_specs=[hbm] * 6,
        out_specs=[vmem] * 3,
        scratch_shapes=[
            pltpu.VMEM(level_table.shape, F32),
            pltpu.VMEM((tokens // HALF, HALF), jnp.int32),
            pltpu.VMEM((tokens // HALF, HALF), jnp.int32),
            pltpu.VMEM((tokens, width), BF16),
            pltpu.VMEM((tokens, width), BF16),
            pltpu.VMEM((2, Z, 16, tokens // 2), BF16),
            pltpu.VMEM((2, Z, 16, tokens // 2), BF16),
            pltpu.VMEM((NT, 32, TILE), BF16),
            pltpu.VMEM((32, 18 * HALF), BF16),
            pltpu.VMEM((NT, TILE, TILE), F32),
            pltpu.VMEM((NT, HALF, TILE), BF16),
            pltpu.VMEM((NT, HALF, WIDTH), F32),
            pltpu.VMEM((NT, HALF, WIDTH), BF16),
            pltpu.VMEM((4, HALF, WIDTH), BF16),
            pltpu.VMEM((HALF, WIDTH), BF16),
            pltpu.VMEM((X, 2, QROWS, WIDTH), BF16),
            pltpu.VMEM((X, TAG, HALF), BF16),
            pltpu.VMEM((Y, TAG, HALF), BF16),
            pltpu.VMEM((X, 2, QROWS, WIDTH), BF16),
            pltpu.VMEM((X, 2, X_LEVELS, QROWS, WIDTH), BF16),
            pltpu.VMEM((2, X, X_LEVELS, QROWS, WIDTH), BF16),
            pltpu.VMEM((2, QROWS, WIDTH), BF16),
            pltpu.VMEM((Y, 2, QROWS, WIDTH), BF16),
            pltpu.VMEM((Y_LEVELS, 2, QROWS, WIDTH), BF16),
            pltpu.VMEM((2, X, Y_LEVELS, QROWS, WIDTH), BF16),
            pltpu.VMEM((X_LEVELS * HALF, WIDTH), BF16),
            pltpu.VMEM((NT, TILE, X_LEVELS * HALF), BF16),
            dma((6,)),
            dma((Z + 1,)),
            dma((Z + 1,)),
            dma((Z,)),
            dma((Z,)),
            dma((Z + 1,)),
            dma((Z + 1,)),
            dma((1,)),
            dma((1,)),
            dma((X,)),
            dma((X,)),
            dma((2 * X,)),
            dma((2 * X,)),
            dma((Y,)),
            dma((Y,)),
            dma((Y_LEVELS * 2 * X,)),
            dma((Y_LEVELS * 2 * X,)),
            dma((X,)),
            dma((X,)),
            dma((Y,)),
            dma((Y,)),
            pltpu.SemaphoreType.REGULAR((2,)),
            dma((1,)),
            dma((1,)),
        ],
        compiler_params=pltpu.CompilerParams(
            collective_id=0, has_side_effects=True, vmem_limit_bytes=40 * 1024 * 1024
        ),
        name="blocks_and_states",
    )(*[pltpu.with_memory_space_constraint(a, pltpu.HBM) for a in arguments])
    return pl.pallas_call(
        last,
        out_shape=jax.ShapeDtypeStruct((tokens, width), BF16),
        in_specs=[vmem] * 3,
        out_specs=pl.BlockSpec(memory_space=pltpu.HBM),
        scratch_shapes=[pltpu.VMEM((tokens, width), BF16), dma((NT,))],
        compiler_params=pltpu.CompilerParams(vmem_limit_bytes=16 * 1024 * 1024),
        name="rows_before",
    )(near, qy, by)


def solution(mesh):
    in_specs = (P("seq", "head"), P("seq", "head"), P("seq", "head"), P(), P("seq"), P("seq"))
    out_specs = P("seq", "head")
    return jax.shard_map(local, mesh=mesh, in_specs=in_specs, out_specs=out_specs, check_vma=False)
```

```python
import jax
import jax.numpy as jnp
from jax import lax
from jax.experimental import pallas as pl
from jax.experimental.pallas import tpu as pltpu
from jax.sharding import PartitionSpec as P

MESH = pl.DeviceIdType.MESH
F32 = jnp.float32
BF16 = jnp.bfloat16

X = 4
Y = 8
Z = 8
TILE = 256
NT = 8
HALF = 128
WIDTH = 256
NEAR_LEVELS = 9
MID_LEVELS = 3
X_LEVELS = 2
Y_LEVELS = 3
FAR_LEVELS = X_LEVELS + Y_LEVELS
LANE = 64
QROWS = 16
TAG = 16
TWO_HOPS = (2, 6, 1, 7)
FARTHEST_FIRST = (4, 3, 5, 2, 6, 1, 7)
DIM0 = (((0,), (0,)), ((), ()))


def dot(a, b):
    return jnp.dot(a, b, preferred_element_type=F32)


def same(a, b):
    return jnp.where(a == b, 1.0, 0.0).astype(F32)


def body(
    k_hbm,
    q_hbm,
    v_hbm,
    tab_hbm,
    cls_hbm,
    doc_hbm,
    near,
    qy,
    by,
    tab_ref,
    cls_ref,
    doc_ref,
    v,
    v_beside,
    kg,
    qg,
    onehot,
    table,
    grid,
    scale,
    kt,
    state,
    left9,
    left10,
    left11,
    tails,
    xtag,
    ytag,
    xbuf,
    xlow,
    xout,
    ysend,
    ybuf,
    ylow,
    yout,
    bx,
    qx,
    in_sem,
    ks_sem,
    kr_sem,
    kps_sem,
    kpr_sem,
    qs_sem,
    qr_sem,
    qps_sem,
    qpr_sem,
    xs_sem,
    xr_sem,
    as_sem,
    ar_sem,
    ys_sem,
    yr_sem,
    bs_sem,
    br_sem,
    ts_sem,
    tr_sem,
    us_sem,
    ur_sem,
    ready_sem,
    vs_sem,
    vr_sem,
):
    seq = lax.axis_index("seq")
    head = lax.axis_index("head")
    x = lax.rem(seq, X)
    y = lax.div(seq, X)
    z = lax.div(head, 2)
    c = lax.rem(head, 2)

    def at_z(d):
        return {"seq": seq, "head": lax.rem(z + d, Z) * 2 + c}

    def at_x(d):
        return {"seq": y * X + lax.rem(x + d, X), "head": head}

    def beside_x(d):
        return {"seq": y * X + lax.rem(x + d, X), "head": z * 2 + (1 - c)}

    def at_y(row):
        return {"seq": row * X + x, "head": head}

    partner = {"seq": seq, "head": z * 2 + (1 - c)}

    def remote(src, dst, send, recv, device):
        return pltpu.make_async_remote_copy(
            src_ref=src,
            dst_ref=dst,
            send_sem=send,
            recv_sem=recv,
            device_id=device,
            device_id_type=MESH,
        )

    barrier = pltpu.get_barrier_semaphore()
    peers = [at_z(d) for d in TWO_HOPS] + [at_x(d) for d in (2, 1, 3)]
    peers = peers + [at_y(lax.rem(y + d, Y)) for d in TWO_HOPS]
    peers = peers + [partner]
    for peer in peers:
        pl.semaphore_signal(barrier, inc=1, device_id=peer, device_id_type=MESH)

    load_k = pltpu.make_async_copy(k_hbm, kg.at[c, z], in_sem.at[0])
    load_q = pltpu.make_async_copy(q_hbm, qg.at[c, z], in_sem.at[1])
    load_v = pltpu.make_async_copy(v_hbm, v, in_sem.at[2])
    load_k.start()
    load_q.start()
    small_loads = [
        pltpu.make_async_copy(tab_hbm, tab_ref, in_sem.at[3]),
        pltpu.make_async_copy(cls_hbm, cls_ref, in_sem.at[4]),
        pltpu.make_async_copy(doc_hbm, doc_ref, in_sem.at[5]),
    ]
    for load in small_loads:
        load.start()
    load_v.start()

    pl.semaphore_wait(barrier, len(peers))

    def gather(shard, slots, send, recv):
        def own(d):
            return remote(shard, slots.at[c, z], send.at[d], recv.at[d], at_z(d))

        def onward(back, hop, index, part):
            slot = slots.at[c, lax.rem(z + Z - back, Z), :, part]
            return remote(slot, slot, send.at[index], recv.at[index], at_z(hop))

        steps = {d: own(d) for d in TWO_HOPS}
        steps[3] = onward(2, 1, 3, pl.ds(0, 1024))
        steps[5] = onward(6, 7, 5, pl.ds(0, 1024))
        steps[4] = onward(2, 2, 4, pl.ds(0, 512))
        steps[8] = onward(6, 6, 8, pl.ds(512, 512))
        return steps

    k_steps = gather(k_hbm, kg, ks_sem, kr_sem)
    q_steps = gather(q_hbm, qg, qs_sem, qr_sem)
    for d in TWO_HOPS:
        k_steps[d].start()

    def k_partner(d):
        slot = kg.at[c, lax.rem(z + Z - d, Z)]
        return remote(slot, slot, kps_sem.at[d], kpr_sem.at[d], partner)

    v_across = remote(v_hbm, v_beside, vs_sem.at[0], vr_sem.at[0], partner)
    v_across.start()
    load_k.wait()
    k_partner(0).start()
    for d in (2, 6):
        row = lax.rem(y + d, Y)
        pl.semaphore_signal(
            ready_sem.at[d // 4], inc=1, device_id=at_y(row), device_id_type=MESH
        )
    for load in small_loads:
        load.wait()
    load_q.wait()

    def last_doc(i):
        return doc_ref[2 * i + 1 : 2 * i + 2, HALF - 1 : HALF].astype(F32)

    xtag[x] = jnp.broadcast_to(last_doc(NT - 1), (TAG, HALF)).astype(BF16)
    t_copies = {}
    for d in (2, 1, 3):
        t_copies[d] = remote(xtag.at[x], xtag.at[x], ts_sem.at[d], tr_sem.at[d], at_x(d))
        t_copies[d].start()

    for order, level in enumerate(list(range(NEAR_LEVELS)) + [None] + list(range(NEAR_LEVELS, 17))):
        columns = slice(order * HALF, (order + 1) * HALF)
        if level is None:
            row = lax.broadcasted_iota(jnp.int32, (32, HALF), 0)
            table[:, columns] = jnp.where(row == 24, 1.0, 0.0).astype(BF16)
        else:
            weight = jnp.broadcast_to(tab_ref[:, level : level + 1], (8, HALF))
            high = weight.astype(BF16).astype(F32)
            middle = (weight - high).astype(BF16).astype(F32)
            low = weight - high - middle
            parts = [high, middle, low, jnp.zeros_like(low)]
            table[:, columns] = jnp.concatenate(parts, axis=0).astype(BF16)

    def doc_row(block):
        return doc_ref[pl.ds(block, 1), :].astype(F32)

    def doc_tile(i):
        return jnp.concatenate([doc_row(2 * i), doc_row(2 * i + 1)], axis=1)

    first_doc = doc_ref[0:1, 0:1].astype(F32)

    def grid_tile(i):
        row8 = lax.broadcasted_iota(jnp.int32, (8, TILE), 0)
        classes = jnp.concatenate(
            [cls_ref[pl.ds(2 * i, 1), :], cls_ref[pl.ds(2 * i + 1, 1), :]], axis=1
        )
        hot = jnp.where(row8 == classes, 1.0, 0.0).astype(F32)
        docs = jnp.where(row8 == 0, doc_tile(i), 0.0)
        onehot[i] = jnp.concatenate([hot, hot, hot, docs], axis=0).astype(BF16)
        wide = lax.dot_general(
            onehot[i], table[:, : 10 * HALF], DIM0, preferred_element_type=F32
        )
        t_pos = lax.broadcasted_iota(jnp.int32, (HALF, HALF), 0)
        s_pos = lax.broadcasted_iota(jnp.int32, (HALF, HALF), 1)
        apart = t_pos ^ s_pos
        causal = s_pos <= t_pos
        for a in range(2):
            rows = slice(a * HALF, (a + 1) * HALF)
            doc_t = wide[rows, 9 * HALF : 10 * HALF]
            weight = wide[rows, :HALF]
            for level in range(1, 8):
                column = wide[rows, level * HALF : (level + 1) * HALF]
                weight = jnp.where(apart >= 1 << (level - 1), column, weight)
            allowed = causal & (doc_t == doc_row(2 * i + a))
            grid[i, rows, rows] = jnp.where(allowed, weight, 0.0)
            if a == 1:
                weight = wide[rows, 8 * HALF : 9 * HALF]
                grid[i, rows, :HALF] = jnp.where(doc_t == doc_row(2 * i), weight, 0.0)
            else:
                grid[i, rows, HALF:] = jnp.zeros((HALF, HALF), F32)
        wide = lax.dot_general(
            onehot[i], table[:, 9 * HALF :], DIM0, preferred_element_type=F32
        )
        doc_t = wide[:, :HALF]
        for b in range(MID_LEVELS + FAR_LEVELS):
            weight = wide[:, (1 + b) * HALF : (2 + b) * HALF]
            if b < MID_LEVELS:
                end = jnp.maximum((i >> b << b) - 1, 0)
                end_doc = doc_row(2 * end + 1)[:, HALF - 1 : HALF]
                present = jnp.where((i >> b) % 2 == 1, 1.0, 0.0).astype(F32)
                weight = jnp.where(doc_t == end_doc, weight * present, 0.0)
            else:
                weight = jnp.where(doc_t == first_doc, weight, 0.0)
            scale[i, :, b * HALF : (b + 1) * HALF] = weight

    @pl.loop(0, NT // 2)
    def _(i):
        grid_tile(i)

    for d, first, second in ((2, 3, 4), (6, 5, 8)):
        k_steps[d].wait_recv()
        k_steps[first].start()
        k_steps[second].start()
    k_partner(2).start()
    k_partner(6).start()
    for d in (1, 7):
        k_steps[d].wait_recv()
        k_partner(d).start()

    for d in TWO_HOPS:
        q_steps[d].start()
    for d in (1, 3, 2):
        t_copies[d].wait_recv()
    ytag[y] = xtag[X - 1]
    for side in range(2):
        pl.semaphore_wait(ready_sem.at[side], 1)

    def u_copy(d):
        row = lax.rem(y + d, Y)
        return remote(ytag.at[y], ytag.at[y], us_sem.at[d], ur_sem.at[d], at_y(row))

    for d in FARTHEST_FIRST:

        @pl.when(y + d < Y)
        def _():
            u_copy(d).start()

    @pl.loop(NT // 2, NT)
    def _(i):
        grid_tile(i)

    by[...] = jnp.zeros_like(by)
    load_v.wait()
    for d in (3, 5):
        k_steps[d].wait_recv()
        k_partner(d).start()
    k_steps[4].wait_recv()
    k_steps[8].wait_recv()
    k_partner(4).start()
    v_across.wait_recv()
    end_doc = last_doc(NT - 1)
    mine = jnp.zeros((LANE, WIDTH), F32)
    theirs = jnp.zeros((LANE, WIDTH), F32)
    for a in range(2):
        keys = kg[c].astype(F32)[:, 8 * a : 8 * a + 8, :]
        docs = jnp.concatenate([doc_row(8 * a + i) for i in range(8)], axis=1)
        kept = jnp.where(docs == end_doc, keys.reshape(LANE, 1024), 0.0).astype(BF16)
        mine = mine + dot(kept, v[a * 1024 : (a + 1) * 1024, :])
        theirs = theirs + dot(kept, v_beside[a * 1024 : (a + 1) * 1024, :])
    for p in range(X):
        tails[p, c] = mine[p * QROWS : (p + 1) * QROWS].astype(BF16)
        tails[p, 1 - c] = theirs[p * QROWS : (p + 1) * QROWS].astype(BF16)

    x_copies = {}
    for d in (2, 1, 3):
        x_copies[d] = remote(
            tails.at[lax.rem(x + d, X)], xbuf.at[x], xs_sem.at[d], xr_sem.at[d], at_x(d)
        )
        x_copies[d].start()
    xbuf[x] = tails[x]
    for d, first, second in ((2, 3, 4), (6, 5, 8)):
        q_steps[d].wait_recv()
        q_steps[first].start()
        q_steps[second].start()

    for d in (0, 2, 6, 1, 7, 3, 5, 4):
        k_partner(d).wait_recv()

    def unpacked(gathered, j):
        wide = gathered[:, :, :, pl.ds(pl.multiple_of(j * TILE, TILE), TILE)].astype(F32)
        return [wide[:, :, 8 * a : 8 * a + 8, :].reshape(HALF, TILE) for a in range(2)]

    @pl.loop(0, NT // 2)
    def _(j):
        for a, keys in enumerate(unpacked(kg, j)):
            i = a * (NT // 2) + j
            docs = doc_tile(i)
            kept = jnp.where(docs == docs[:, TILE - 1 : TILE], keys, 0.0)
            kt[i] = keys.astype(BF16)
            part = dot(kept.astype(BF16), v[pl.ds(pl.multiple_of(i * TILE, TILE), TILE), :])
            state[i] = part
            left9[i] = part.astype(BF16)

    level_states = [state[i] for i in range(NT)]
    pairs = [
        level_states[2 * j + 1] + same(last_doc(2 * j), last_doc(2 * j + 1)) * level_states[2 * j]
        for j in range(4)
    ]
    for j in range(4):
        left10[j] = pairs[j].astype(BF16)
    first_quad = pairs[1] + same(last_doc(1), last_doc(3)) * pairs[0]
    left11[...] = first_quad.astype(BF16)

    for d in (1, 3, 2):
        x_copies[d].wait_recv()
    ends = [xtag[p].astype(F32)[0:1, 0:1] for p in range(X)]
    terms = [xbuf[p].astype(F32) for p in range(X)]
    low_pair = terms[1] + same(ends[0], ends[1]) * terms[0]
    high_pair = terms[3] + same(ends[2], ends[3]) * terms[2]
    row_tail = high_pair + same(ends[1], ends[3]) * low_pair
    ysend[...] = row_tail.astype(BF16)

    def y_copy(d):
        row = lax.rem(y + d, Y)
        return remote(ysend, ybuf.at[y], ys_sem.at[d], yr_sem.at[d], at_y(row))

    for d in FARTHEST_FIRST:

        @pl.when(y + d < Y)
        def _():
            y_copy(d).start()

    blank = jnp.zeros((2, QROWS, WIDTH), BF16)
    low = low_pair.astype(BF16)
    pieces = [(blank, blank), (xbuf[0], blank), (blank, low), (xbuf[2], low)]
    for p in range(X):
        for b in range(X_LEVELS):
            for core in range(2):
                xlow[p, core, b] = pieces[p][b][core]

    def fan_out(make):
        return [make(d, d, at_x(d), c) for d in (2, 1, 3)] + [
            make(d, X + d, beside_x(d), 1 - c) for d in (2, 1, 3, 0)
        ]

    def a_copy(d, index, device, core):
        source = xlow.at[lax.rem(x + d, X), core]
        return remote(source, xout.at[c, x], as_sem.at[index], ar_sem.at[index], device)

    a_copies = fan_out(a_copy)
    for copy in a_copies:
        copy.start()
    xout[c, x] = xlow[x, c]

    for d in (1, 7, 3, 5, 4, 8):
        q_steps[d].wait_recv()
    q_partner = remote(qg.at[c], qg.at[c], qps_sem.at[0], qpr_sem.at[0], partner)
    q_partner.start()

    q_partner.wait_recv()

    def near_tile(i, queries):
        turned = queries.T
        rows = pl.ds(pl.multiple_of(i * TILE, TILE), TILE)
        scores = dot(turned.astype(BF16), kt[i])
        weighted = (scores * grid[i]).astype(BF16)
        total = dot(weighted, v[rows, :])
        mids = []
        for b in range(MID_LEVELS):
            mids.append((scale[i, :, b * HALF : (b + 1) * HALF] * turned).astype(BF16))
        lefts = [
            left9[jnp.maximum(i - 1, 0)],
            left10[jnp.maximum((i >> 1) - 1, 0)],
            left11[...],
        ]
        total = total + dot(jnp.concatenate(mids, axis=1), jnp.concatenate(lefts, axis=0))
        near[i] = total
        for b in range(FAR_LEVELS):
            start = (MID_LEVELS + b) * HALF
            target, place = (qx, b) if b < X_LEVELS else (qy, b - X_LEVELS)
            columns = slice(place * HALF, (place + 1) * HALF)
            target[i, :, columns] = (scale[i, :, start : start + HALF] * turned).astype(BF16)

    @pl.loop(0, NT // 4)
    def _(j):
        for a, queries in enumerate(unpacked(qg, j)):
            near_tile(a * (NT // 2) + j, queries)

    for d in range(1, Y):

        @pl.when(y >= d)
        def _():
            u_copy(d).wait_recv()

    def y_row(row):
        return ybuf[row].astype(F32)

    def y_end(row):
        return ytag[row].astype(F32)[0:1, 0:1]

    def b_copies(b):
        def b_copy(d, index, device, core):
            send, recv = bs_sem.at[b * 2 * X + index], br_sem.at[b * 2 * X + index]
            return remote(ylow.at[b, core], yout.at[c, x, b], send, recv, device)

        return fan_out(b_copy)

    def hand_on(b, merged):
        ylow[b] = merged
        for copy in b_copies(b):
            copy.start()
        yout[c, x, b] = ylow[b, c]

    bits = [lax.rem(y, 2) == 1, lax.rem(lax.div(y, 2), 2) == 1, y >= 4]
    four = lax.div(y, 4) * 4

    @pl.when(bits[0])
    def _():
        y_copy(1).wait_recv()
        hand_on(0, ybuf[y - 1])

    @pl.when(bits[1])
    def _():
        for d in range(2):
            y_copy(y - four - d).wait_recv()
        merged = y_row(four + 1) + same(y_end(four), y_end(four + 1)) * y_row(four)
        hand_on(1, merged.astype(BF16))

    @pl.when(bits[2])
    def _():
        for d in range(4):
            y_copy(y - d).wait_recv()
        early = y_row(1) + same(y_end(0), y_end(1)) * y_row(0)
        late = y_row(3) + same(y_end(2), y_end(3)) * y_row(2)
        merged = late + same(y_end(1), y_end(3)) * early
        hand_on(2, merged.astype(BF16))

    @pl.loop(NT // 4, NT // 2)
    def _(j):
        for a, queries in enumerate(unpacked(qg, j)):
            near_tile(a * (NT // 2) + j, queries)

    for copy in a_copies:
        copy.wait_recv()
    before = xtag[jnp.maximum(x - 1, 0)].astype(F32)[0:1, 0:1]
    x_masks = [same(before, first_doc), same(ends[1], first_doc)]
    for b in range(2):
        rows = xout[:, :, b].astype(F32).reshape(HALF, WIDTH)
        bx[b * HALF : (b + 1) * HALF] = (rows * x_masks[b]).astype(BF16)

    @pl.loop(0, NT // 2)
    def _(j):
        for i in (2 * j, 2 * j + 1):
            near[i] = near[i] + dot(qx[i], bx[...])

    y_ends = [y - 1, four + 1, 3]
    for b in range(Y_LEVELS):

        @pl.when(bits[b])
        def _():
            for copy in b_copies(b):
                copy.wait_recv()
            rows = yout[:, :, b].astype(F32).reshape(HALF, WIDTH)
            mask = same(y_end(y_ends[b]), first_doc)
            by[b * HALF : (b + 1) * HALF] = (rows * mask).astype(BF16)

    for step in k_steps:
        k_steps[step].wait_send()
        q_steps[step].wait_send()
    for d in range(Z):
        k_partner(d).wait_send()
    q_partner.wait_send()
    v_across.wait_send()
    for d in range(1, X):
        t_copies[d].wait_send()
        x_copies[d].wait_send()
    for copy in a_copies:
        copy.wait_send()
    for b in range(Y_LEVELS):

        @pl.when(bits[b])
        def _():
            for copy in b_copies(b):
                copy.wait_send()

    for d in range(1, Y):

        @pl.when(y + d < Y)
        def _():
            u_copy(d).wait_send()
            y_copy(d).wait_send()


def last(near, qy, by, out_hbm, out, out_sem):
    copies = []
    for i in range(NT):
        rows = pl.ds(i * TILE, TILE)
        out[rows, :] = (near[i] + dot(qy[i], by[...])).astype(BF16)
        copies.append(pltpu.make_async_copy(out.at[rows], out_hbm.at[rows], out_sem.at[i]))
        copies[i].start()
    for copy in copies:
        copy.wait()


def folded(shard):
    tokens, width = shard.shape
    return shard.T.reshape(width, 2, tokens // 2).swapaxes(0, 1).reshape(2 * width, tokens // 2)


def local(queries, key_vectors, values, level_table, level_class, doc_ids):
    tokens, width = values.shape
    vmem = pl.BlockSpec(memory_space=pltpu.VMEM)
    hbm = pl.BlockSpec(memory_space=pltpu.HBM)
    dma = pltpu.SemaphoreType.DMA
    arguments = (
        folded(key_vectors),
        folded(queries),
        values,
        level_table,
        level_class.reshape(tokens // HALF, HALF),
        doc_ids.reshape(tokens // HALF, HALF),
    )
    near, qy, by = pl.pallas_call(
        body,
        out_shape=[
            pltpu.VMEM((NT, TILE, WIDTH), F32),
            pltpu.VMEM((NT, TILE, Y_LEVELS * HALF), BF16),
            pltpu.VMEM((Y_LEVELS * HALF, WIDTH), BF16),
        ],
        in_specs=[hbm] * 6,
        out_specs=[vmem] * 3,
        scratch_shapes=[
            pltpu.VMEM(level_table.shape, F32),
            pltpu.VMEM((tokens // HALF, HALF), jnp.int32),
            pltpu.VMEM((tokens // HALF, HALF), jnp.int32),
            pltpu.VMEM((tokens, width), BF16),
            pltpu.VMEM((tokens, width), BF16),
            pltpu.VMEM((2, Z, 16, tokens // 2), BF16),
            pltpu.VMEM((2, Z, 16, tokens // 2), BF16),
            pltpu.VMEM((NT, 32, TILE), BF16),
            pltpu.VMEM((32, 18 * HALF), BF16),
            pltpu.VMEM((NT, TILE, TILE), F32),
            pltpu.VMEM((NT, TILE, (MID_LEVELS + FAR_LEVELS) * HALF), F32),
            pltpu.VMEM((NT, HALF, TILE), BF16),
            pltpu.VMEM((NT, HALF, WIDTH), F32),
            pltpu.VMEM((NT, HALF, WIDTH), BF16),
            pltpu.VMEM((4, HALF, WIDTH), BF16),
            pltpu.VMEM((HALF, WIDTH), BF16),
            pltpu.VMEM((X, 2, QROWS, WIDTH), BF16),
            pltpu.VMEM((X, TAG, HALF), BF16),
            pltpu.VMEM((Y, TAG, HALF), BF16),
            pltpu.VMEM((X, 2, QROWS, WIDTH), BF16),
            pltpu.VMEM((X, 2, X_LEVELS, QROWS, WIDTH), BF16),
            pltpu.VMEM((2, X, X_LEVELS, QROWS, WIDTH), BF16),
            pltpu.VMEM((2, QROWS, WIDTH), BF16),
            pltpu.VMEM((Y, 2, QROWS, WIDTH), BF16),
            pltpu.VMEM((Y_LEVELS, 2, QROWS, WIDTH), BF16),
            pltpu.VMEM((2, X, Y_LEVELS, QROWS, WIDTH), BF16),
            pltpu.VMEM((X_LEVELS * HALF, WIDTH), BF16),
            pltpu.VMEM((NT, TILE, X_LEVELS * HALF), BF16),
            dma((6,)),
            dma((Z + 1,)),
            dma((Z + 1,)),
            dma((Z,)),
            dma((Z,)),
            dma((Z + 1,)),
            dma((Z + 1,)),
            dma((1,)),
            dma((1,)),
            dma((X,)),
            dma((X,)),
            dma((2 * X,)),
            dma((2 * X,)),
            dma((Y,)),
            dma((Y,)),
            dma((Y_LEVELS * 2 * X,)),
            dma((Y_LEVELS * 2 * X,)),
            dma((X,)),
            dma((X,)),
            dma((Y,)),
            dma((Y,)),
            pltpu.SemaphoreType.REGULAR((2,)),
            dma((1,)),
            dma((1,)),
        ],
        compiler_params=pltpu.CompilerParams(
            collective_id=0, has_side_effects=True, vmem_limit_bytes=40 * 1024 * 1024
        ),
        name="blocks_and_states",
    )(*[pltpu.with_memory_space_constraint(a, pltpu.HBM) for a in arguments])
    return pl.pallas_call(
        last,
        out_shape=jax.ShapeDtypeStruct((tokens, width), BF16),
        in_specs=[vmem] * 3,
        out_specs=pl.BlockSpec(memory_space=pltpu.HBM),
        scratch_shapes=[pltpu.VMEM((tokens, width), BF16), dma((NT,))],
        compiler_params=pltpu.CompilerParams(vmem_limit_bytes=16 * 1024 * 1024),
        name="rows_before",
    )(near, qy, by)


def solution(mesh):
    in_specs = (P("seq", "head"), P("seq", "head"), P("seq", "head"), P(), P("seq"), P("seq"))
    out_specs = P("seq", "head")
    return jax.shard_map(local, mesh=mesh, in_specs=in_specs, out_specs=out_specs, check_vma=False)
```

```python
import jax
import jax.numpy as jnp
from jax import lax
from jax.experimental import pallas as pl
from jax.experimental.pallas import tpu as pltpu
from jax.sharding import PartitionSpec as P

MESH = pl.DeviceIdType.MESH
F32 = jnp.float32
BF16 = jnp.bfloat16

X = 4
Y = 8
Z = 8
TILE = 256
NT = 8
HALF = 128
WIDTH = 256
NEAR_LEVELS = 9
MID_LEVELS = 3
X_LEVELS = 2
Y_LEVELS = 3
FAR_LEVELS = X_LEVELS + Y_LEVELS
LANE = 64
QROWS = 16
TAG = 16
TWO_HOPS = (2, 6, 1, 7)
FARTHEST_FIRST = (4, 3, 5, 2, 6, 1, 7)
DIM0 = (((0,), (0,)), ((), ()))


def dot(a, b):
    return jnp.dot(a, b, preferred_element_type=F32)


def same(a, b):
    return jnp.where(a == b, 1.0, 0.0).astype(F32)


def body(
    k_hbm,
    q_hbm,
    v_hbm,
    tab_hbm,
    cls_hbm,
    doc_hbm,
    near,
    qy,
    by,
    tab_ref,
    cls_ref,
    doc_ref,
    v,
    v_beside,
    kg,
    qg,
    onehot,
    table,
    grid,
    scale,
    kt,
    state,
    left9,
    left10,
    left11,
    tails,
    xtag,
    ytag,
    xbuf,
    xlow,
    xout,
    ysend,
    ybuf,
    ylow,
    yout,
    bx,
    qx,
    in_sem,
    ks_sem,
    kr_sem,
    kps_sem,
    kpr_sem,
    qs_sem,
    qr_sem,
    qps_sem,
    qpr_sem,
    xs_sem,
    xr_sem,
    as_sem,
    ar_sem,
    ys_sem,
    yr_sem,
    bs_sem,
    br_sem,
    ts_sem,
    tr_sem,
    us_sem,
    ur_sem,
    ready_sem,
    vs_sem,
    vr_sem,
):
    seq = lax.axis_index("seq")
    head = lax.axis_index("head")
    x = lax.rem(seq, X)
    y = lax.div(seq, X)
    z = lax.div(head, 2)
    c = lax.rem(head, 2)

    def at_z(d):
        return {"seq": seq, "head": lax.rem(z + d, Z) * 2 + c}

    def at_x(d):
        return {"seq": y * X + lax.rem(x + d, X), "head": head}

    def beside_x(d):
        return {"seq": y * X + lax.rem(x + d, X), "head": z * 2 + (1 - c)}

    def at_y(row):
        return {"seq": row * X + x, "head": head}

    partner = {"seq": seq, "head": z * 2 + (1 - c)}

    def remote(src, dst, send, recv, device):
        return pltpu.make_async_remote_copy(
            src_ref=src,
            dst_ref=dst,
            send_sem=send,
            recv_sem=recv,
            device_id=device,
            device_id_type=MESH,
        )

    barrier = pltpu.get_barrier_semaphore()
    peers = [at_z(d) for d in TWO_HOPS] + [at_x(d) for d in (2, 1, 3)]
    peers = peers + [at_y(lax.rem(y + d, Y)) for d in TWO_HOPS]
    peers = peers + [partner]
    for peer in peers:
        pl.semaphore_signal(barrier, inc=1, device_id=peer, device_id_type=MESH)

    load_k = pltpu.make_async_copy(k_hbm, kg.at[c, z], in_sem.at[0])
    load_q = pltpu.make_async_copy(q_hbm, qg.at[c, z], in_sem.at[1])
    load_v = pltpu.make_async_copy(v_hbm, v, in_sem.at[2])
    load_k.start()
    load_q.start()
    small_loads = [
        pltpu.make_async_copy(tab_hbm, tab_ref, in_sem.at[3]),
        pltpu.make_async_copy(cls_hbm, cls_ref, in_sem.at[4]),
        pltpu.make_async_copy(doc_hbm, doc_ref, in_sem.at[5]),
    ]
    for load in small_loads:
        load.start()
    load_v.start()

    pl.semaphore_wait(barrier, len(peers))

    def gather(shard, slots, send, recv):
        def own(d):
            return remote(shard, slots.at[c, z], send.at[d], recv.at[d], at_z(d))

        def onward(back, hop, index, part):
            slot = slots.at[c, lax.rem(z + Z - back, Z), :, part]
            return remote(slot, slot, send.at[index], recv.at[index], at_z(hop))

        steps = {d: own(d) for d in TWO_HOPS}
        steps[3] = onward(2, 1, 3, pl.ds(0, 1024))
        steps[5] = onward(6, 7, 5, pl.ds(0, 1024))
        steps[4] = onward(2, 2, 4, pl.ds(0, 512))
        steps[8] = onward(6, 6, 8, pl.ds(512, 512))
        return steps

    def half(h):
        return pl.ds(512 * h, 512)

    def k_own(d, h):
        slot = kg.at[c, z, :, half(h)]
        index = 2 * d + h
        return remote(k_hbm.at[:, half(h)], slot, ks_sem.at[index], kr_sem.at[index], at_z(d))

    def k_onward(back, hop, d, h):
        slot = kg.at[c, lax.rem(z + Z - back, Z), :, half(h)]
        index = 2 * d + h
        return remote(slot, slot, ks_sem.at[index], kr_sem.at[index], at_z(hop))

    k_steps = {(d, h): k_own(d, h) for d in TWO_HOPS for h in range(2)}
    for h in range(2):
        k_steps[3, h] = k_onward(2, 1, 3, h)
        k_steps[5, h] = k_onward(6, 7, 5, h)
    k_steps[4, 0] = k_onward(2, 2, 4, 0)
    k_steps[4, 1] = k_onward(6, 6, 4, 1)
    q_steps = gather(q_hbm, qg, qs_sem, qr_sem)
    for step in ((2, 0), (6, 1), (2, 1), (6, 0), (1, 0), (7, 1), (1, 1), (7, 0)):
        k_steps[step].start()

    def k_partner(d):
        slot = kg.at[c, lax.rem(z + Z - d, Z)]
        return remote(slot, slot, kps_sem.at[d], kpr_sem.at[d], partner)

    v_across = remote(v_hbm, v_beside, vs_sem.at[0], vr_sem.at[0], partner)
    v_across.start()
    load_k.wait()
    k_partner(0).start()
    for d in (2, 6):
        row = lax.rem(y + d, Y)
        pl.semaphore_signal(
            ready_sem.at[d // 4], inc=1, device_id=at_y(row), device_id_type=MESH
        )
    for load in small_loads:
        load.wait()
    load_q.wait()

    def last_doc(i):
        return doc_ref[2 * i + 1 : 2 * i + 2, HALF - 1 : HALF].astype(F32)

    xtag[x] = jnp.broadcast_to(last_doc(NT - 1), (TAG, HALF)).astype(BF16)
    t_copies = {}
    for d in (2, 1, 3):
        t_copies[d] = remote(xtag.at[x], xtag.at[x], ts_sem.at[d], tr_sem.at[d], at_x(d))
        t_copies[d].start()

    for order, level in enumerate(list(range(NEAR_LEVELS)) + [None] + list(range(NEAR_LEVELS, 17))):
        columns = slice(order * HALF, (order + 1) * HALF)
        if level is None:
            row = lax.broadcasted_iota(jnp.int32, (32, HALF), 0)
            table[:, columns] = jnp.where(row == 24, 1.0, 0.0).astype(BF16)
        else:
            weight = jnp.broadcast_to(tab_ref[:, level : level + 1], (8, HALF))
            high = weight.astype(BF16).astype(F32)
            middle = (weight - high).astype(BF16).astype(F32)
            low = weight - high - middle
            parts = [high, middle, low, jnp.zeros_like(low)]
            table[:, columns] = jnp.concatenate(parts, axis=0).astype(BF16)

    def doc_row(block):
        return doc_ref[pl.ds(block, 1), :].astype(F32)

    def doc_tile(i):
        return jnp.concatenate([doc_row(2 * i), doc_row(2 * i + 1)], axis=1)

    first_doc = doc_ref[0:1, 0:1].astype(F32)

    def grid_tile(i):
        row8 = lax.broadcasted_iota(jnp.int32, (8, TILE), 0)
        classes = jnp.concatenate(
            [cls_ref[pl.ds(2 * i, 1), :], cls_ref[pl.ds(2 * i + 1, 1), :]], axis=1
        )
        hot = jnp.where(row8 == classes, 1.0, 0.0).astype(F32)
        docs = jnp.where(row8 == 0, doc_tile(i), 0.0)
        onehot[i] = jnp.concatenate([hot, hot, hot, docs], axis=0).astype(BF16)
        wide = lax.dot_general(
            onehot[i], table[:, : 10 * HALF], DIM0, preferred_element_type=F32
        )
        t_pos = lax.broadcasted_iota(jnp.int32, (HALF, HALF), 0)
        s_pos = lax.broadcasted_iota(jnp.int32, (HALF, HALF), 1)
        apart = t_pos ^ s_pos
        causal = s_pos <= t_pos
        for a in range(2):
            rows = slice(a * HALF, (a + 1) * HALF)
            doc_t = wide[rows, 9 * HALF : 10 * HALF]
            weight = wide[rows, :HALF]
            for level in range(1, 8):
                column = wide[rows, level * HALF : (level + 1) * HALF]
                weight = jnp.where(apart >= 1 << (level - 1), column, weight)
            allowed = causal & (doc_t == doc_row(2 * i + a))
            grid[i, rows, rows] = jnp.where(allowed, weight, 0.0)
            if a == 1:
                weight = wide[rows, 8 * HALF : 9 * HALF]
                grid[i, rows, :HALF] = jnp.where(doc_t == doc_row(2 * i), weight, 0.0)
            else:
                grid[i, rows, HALF:] = jnp.zeros((HALF, HALF), F32)
        wide = lax.dot_general(
            onehot[i], table[:, 9 * HALF :], DIM0, preferred_element_type=F32
        )
        doc_t = wide[:, :HALF]
        for b in range(MID_LEVELS + FAR_LEVELS):
            weight = wide[:, (1 + b) * HALF : (2 + b) * HALF]
            if b < MID_LEVELS:
                end = jnp.maximum((i >> b << b) - 1, 0)
                end_doc = doc_row(2 * end + 1)[:, HALF - 1 : HALF]
                present = jnp.where((i >> b) % 2 == 1, 1.0, 0.0).astype(F32)
                weight = jnp.where(doc_t == end_doc, weight * present, 0.0)
            else:
                weight = jnp.where(doc_t == first_doc, weight, 0.0)
            scale[i, :, b * HALF : (b + 1) * HALF] = weight

    @pl.loop(0, NT // 2)
    def _(i):
        grid_tile(i)

    onwards = {(2, 0): [(4, 0), (3, 0)], (6, 1): [(4, 1), (5, 1)], (2, 1): [(3, 1)], (6, 0): [(5, 0)]}
    for step, following in onwards.items():
        k_steps[step].wait_recv()
        for other in following:
            k_steps[other].start()
    k_partner(2).start()
    k_partner(6).start()
    for d in (1, 7):
        for h in range(2):
            k_steps[d, h].wait_recv()
        k_partner(d).start()

    for d in TWO_HOPS:
        q_steps[d].start()
    for d in (1, 3, 2):
        t_copies[d].wait_recv()
    ytag[y] = xtag[X - 1]
    for side in range(2):
        pl.semaphore_wait(ready_sem.at[side], 1)

    def u_copy(d):
        row = lax.rem(y + d, Y)
        return remote(ytag.at[y], ytag.at[y], us_sem.at[d], ur_sem.at[d], at_y(row))

    for d in FARTHEST_FIRST:

        @pl.when(y + d < Y)
        def _():
            u_copy(d).start()

    @pl.loop(NT // 2, NT)
    def _(i):
        grid_tile(i)

    by[...] = jnp.zeros_like(by)
    load_v.wait()
    for d in (3, 5, 4):
        for h in range(2):
            k_steps[d, h].wait_recv()
        k_partner(d).start()
    v_across.wait_recv()
    end_doc = last_doc(NT - 1)
    mine = jnp.zeros((LANE, WIDTH), F32)
    theirs = jnp.zeros((LANE, WIDTH), F32)
    for a in range(2):
        keys = kg[c].astype(F32)[:, 8 * a : 8 * a + 8, :]
        docs = jnp.concatenate([doc_row(8 * a + i) for i in range(8)], axis=1)
        kept = jnp.where(docs == end_doc, keys.reshape(LANE, 1024), 0.0).astype(BF16)
        mine = mine + dot(kept, v[a * 1024 : (a + 1) * 1024, :])
        theirs = theirs + dot(kept, v_beside[a * 1024 : (a + 1) * 1024, :])
    for p in range(X):
        tails[p, c] = mine[p * QROWS : (p + 1) * QROWS].astype(BF16)
        tails[p, 1 - c] = theirs[p * QROWS : (p + 1) * QROWS].astype(BF16)

    x_copies = {}
    for d in (2, 1, 3):
        x_copies[d] = remote(
            tails.at[lax.rem(x + d, X)], xbuf.at[x], xs_sem.at[d], xr_sem.at[d], at_x(d)
        )
        x_copies[d].start()
    xbuf[x] = tails[x]
    for d, first, second in ((2, 3, 4), (6, 5, 8)):
        q_steps[d].wait_recv()
        q_steps[first].start()
        q_steps[second].start()

    for d in (0, 2, 6, 1, 7, 3, 5, 4):
        k_partner(d).wait_recv()

    def unpacked(gathered, j):
        wide = gathered[:, :, :, pl.ds(pl.multiple_of(j * TILE, TILE), TILE)].astype(F32)
        return [wide[:, :, 8 * a : 8 * a + 8, :].reshape(HALF, TILE) for a in range(2)]

    @pl.loop(0, NT // 2)
    def _(j):
        for a, keys in enumerate(unpacked(kg, j)):
            i = a * (NT // 2) + j
            docs = doc_tile(i)
            kept = jnp.where(docs == docs[:, TILE - 1 : TILE], keys, 0.0)
            kt[i] = keys.astype(BF16)
            part = dot(kept.astype(BF16), v[pl.ds(pl.multiple_of(i * TILE, TILE), TILE), :])
            state[i] = part
            left9[i] = part.astype(BF16)

    level_states = [state[i] for i in range(NT)]
    pairs = [
        level_states[2 * j + 1] + same(last_doc(2 * j), last_doc(2 * j + 1)) * level_states[2 * j]
        for j in range(4)
    ]
    for j in range(4):
        left10[j] = pairs[j].astype(BF16)
    first_quad = pairs[1] + same(last_doc(1), last_doc(3)) * pairs[0]
    left11[...] = first_quad.astype(BF16)

    for d in (1, 3, 2):
        x_copies[d].wait_recv()
    ends = [xtag[p].astype(F32)[0:1, 0:1] for p in range(X)]
    terms = [xbuf[p].astype(F32) for p in range(X)]
    low_pair = terms[1] + same(ends[0], ends[1]) * terms[0]
    high_pair = terms[3] + same(ends[2], ends[3]) * terms[2]
    row_tail = high_pair + same(ends[1], ends[3]) * low_pair
    ysend[...] = row_tail.astype(BF16)

    def y_copy(d):
        row = lax.rem(y + d, Y)
        return remote(ysend, ybuf.at[y], ys_sem.at[d], yr_sem.at[d], at_y(row))

    for d in FARTHEST_FIRST:

        @pl.when(y + d < Y)
        def _():
            y_copy(d).start()

    blank = jnp.zeros((2, QROWS, WIDTH), BF16)
    low = low_pair.astype(BF16)
    pieces = [(blank, blank), (xbuf[0], blank), (blank, low), (xbuf[2], low)]
    for p in range(X):
        for b in range(X_LEVELS):
            for core in range(2):
                xlow[p, core, b] = pieces[p][b][core]

    def fan_out(make):
        return [make(d, d, at_x(d), c) for d in (2, 1, 3)] + [
            make(d, X + d, beside_x(d), 1 - c) for d in (2, 1, 3, 0)
        ]

    def a_copy(d, index, device, core):
        source = xlow.at[lax.rem(x + d, X), core]
        return remote(source, xout.at[c, x], as_sem.at[index], ar_sem.at[index], device)

    a_copies = fan_out(a_copy)
    for copy in a_copies:
        copy.start()
    xout[c, x] = xlow[x, c]

    for d in (1, 7, 3, 5, 4, 8):
        q_steps[d].wait_recv()
    q_partner = remote(qg.at[c], qg.at[c], qps_sem.at[0], qpr_sem.at[0], partner)
    q_partner.start()

    q_partner.wait_recv()

    def near_tile(i, queries):
        turned = queries.T
        rows = pl.ds(pl.multiple_of(i * TILE, TILE), TILE)
        scores = dot(turned.astype(BF16), kt[i])
        weighted = (scores * grid[i]).astype(BF16)
        total = dot(weighted, v[rows, :])
        mids = []
        for b in range(MID_LEVELS):
            mids.append((scale[i, :, b * HALF : (b + 1) * HALF] * turned).astype(BF16))
        lefts = [
            left9[jnp.maximum(i - 1, 0)],
            left10[jnp.maximum((i >> 1) - 1, 0)],
            left11[...],
        ]
        total = total + dot(jnp.concatenate(mids, axis=1), jnp.concatenate(lefts, axis=0))
        near[i] = total
        for b in range(FAR_LEVELS):
            start = (MID_LEVELS + b) * HALF
            target, place = (qx, b) if b < X_LEVELS else (qy, b - X_LEVELS)
            columns = slice(place * HALF, (place + 1) * HALF)
            target[i, :, columns] = (scale[i, :, start : start + HALF] * turned).astype(BF16)

    @pl.loop(0, NT // 4)
    def _(j):
        for a, queries in enumerate(unpacked(qg, j)):
            near_tile(a * (NT // 2) + j, queries)

    for d in range(1, Y):

        @pl.when(y >= d)
        def _():
            u_copy(d).wait_recv()

    def y_row(row):
        return ybuf[row].astype(F32)

    def y_end(row):
        return ytag[row].astype(F32)[0:1, 0:1]

    def b_copies(b):
        def b_copy(d, index, device, core):
            send, recv = bs_sem.at[b * 2 * X + index], br_sem.at[b * 2 * X + index]
            return remote(ylow.at[b, core], yout.at[c, x, b], send, recv, device)

        return fan_out(b_copy)

    def hand_on(b, merged):
        ylow[b] = merged
        for copy in b_copies(b):
            copy.start()
        yout[c, x, b] = ylow[b, c]

    bits = [lax.rem(y, 2) == 1, lax.rem(lax.div(y, 2), 2) == 1, y >= 4]
    four = lax.div(y, 4) * 4

    @pl.when(bits[0])
    def _():
        y_copy(1).wait_recv()
        hand_on(0, ybuf[y - 1])

    @pl.when(bits[1])
    def _():
        for d in range(2):
            y_copy(y - four - d).wait_recv()
        merged = y_row(four + 1) + same(y_end(four), y_end(four + 1)) * y_row(four)
        hand_on(1, merged.astype(BF16))

    @pl.when(bits[2])
    def _():
        for d in range(4):
            y_copy(y - d).wait_recv()
        early = y_row(1) + same(y_end(0), y_end(1)) * y_row(0)
        late = y_row(3) + same(y_end(2), y_end(3)) * y_row(2)
        merged = late + same(y_end(1), y_end(3)) * early
        hand_on(2, merged.astype(BF16))

    @pl.loop(NT // 4, NT // 2)
    def _(j):
        for a, queries in enumerate(unpacked(qg, j)):
            near_tile(a * (NT // 2) + j, queries)

    for copy in a_copies:
        copy.wait_recv()
    before = xtag[jnp.maximum(x - 1, 0)].astype(F32)[0:1, 0:1]
    x_masks = [same(before, first_doc), same(ends[1], first_doc)]
    for b in range(2):
        rows = xout[:, :, b].astype(F32).reshape(HALF, WIDTH)
        bx[b * HALF : (b + 1) * HALF] = (rows * x_masks[b]).astype(BF16)

    @pl.loop(0, NT // 2)
    def _(j):
        for i in (2 * j, 2 * j + 1):
            near[i] = near[i] + dot(qx[i], bx[...])

    y_ends = [y - 1, four + 1, 3]
    for b in range(Y_LEVELS):

        @pl.when(bits[b])
        def _():
            for copy in b_copies(b):
                copy.wait_recv()
            rows = yout[:, :, b].astype(F32).reshape(HALF, WIDTH)
            mask = same(y_end(y_ends[b]), first_doc)
            by[b * HALF : (b + 1) * HALF] = (rows * mask).astype(BF16)

    for step in k_steps:
        k_steps[step].wait_send()
    for step in q_steps:
        q_steps[step].wait_send()
    for d in range(Z):
        k_partner(d).wait_send()
    q_partner.wait_send()
    v_across.wait_send()
    for d in range(1, X):
        t_copies[d].wait_send()
        x_copies[d].wait_send()
    for copy in a_copies:
        copy.wait_send()
    for b in range(Y_LEVELS):

        @pl.when(bits[b])
        def _():
            for copy in b_copies(b):
                copy.wait_send()

    for d in range(1, Y):

        @pl.when(y + d < Y)
        def _():
            u_copy(d).wait_send()
            y_copy(d).wait_send()


def last(near, qy, by, out_hbm, out, out_sem):
    copies = []
    for i in range(NT):
        rows = pl.ds(i * TILE, TILE)
        out[rows, :] = (near[i] + dot(qy[i], by[...])).astype(BF16)
        copies.append(pltpu.make_async_copy(out.at[rows], out_hbm.at[rows], out_sem.at[i]))
        copies[i].start()
    for copy in copies:
        copy.wait()


def folded(shard):
    tokens, width = shard.shape
    return shard.T.reshape(width, 2, tokens // 2).swapaxes(0, 1).reshape(2 * width, tokens // 2)


def local(queries, key_vectors, values, level_table, level_class, doc_ids):
    tokens, width = values.shape
    vmem = pl.BlockSpec(memory_space=pltpu.VMEM)
    hbm = pl.BlockSpec(memory_space=pltpu.HBM)
    dma = pltpu.SemaphoreType.DMA
    arguments = (
        folded(key_vectors),
        folded(queries),
        values,
        level_table,
        level_class.reshape(tokens // HALF, HALF),
        doc_ids.reshape(tokens // HALF, HALF),
    )
    near, qy, by = pl.pallas_call(
        body,
        out_shape=[
            pltpu.VMEM((NT, TILE, WIDTH), F32),
            pltpu.VMEM((NT, TILE, Y_LEVELS * HALF), BF16),
            pltpu.VMEM((Y_LEVELS * HALF, WIDTH), BF16),
        ],
        in_specs=[hbm] * 6,
        out_specs=[vmem] * 3,
        scratch_shapes=[
            pltpu.VMEM(level_table.shape, F32),
            pltpu.VMEM((tokens // HALF, HALF), jnp.int32),
            pltpu.VMEM((tokens // HALF, HALF), jnp.int32),
            pltpu.VMEM((tokens, width), BF16),
            pltpu.VMEM((tokens, width), BF16),
            pltpu.VMEM((2, Z, 16, tokens // 2), BF16),
            pltpu.VMEM((2, Z, 16, tokens // 2), BF16),
            pltpu.VMEM((NT, 32, TILE), BF16),
            pltpu.VMEM((32, 18 * HALF), BF16),
            pltpu.VMEM((NT, TILE, TILE), F32),
            pltpu.VMEM((NT, TILE, (MID_LEVELS + FAR_LEVELS) * HALF), F32),
            pltpu.VMEM((NT, HALF, TILE), BF16),
            pltpu.VMEM((NT, HALF, WIDTH), F32),
            pltpu.VMEM((NT, HALF, WIDTH), BF16),
            pltpu.VMEM((4, HALF, WIDTH), BF16),
            pltpu.VMEM((HALF, WIDTH), BF16),
            pltpu.VMEM((X, 2, QROWS, WIDTH), BF16),
            pltpu.VMEM((X, TAG, HALF), BF16),
            pltpu.VMEM((Y, TAG, HALF), BF16),
            pltpu.VMEM((X, 2, QROWS, WIDTH), BF16),
            pltpu.VMEM((X, 2, X_LEVELS, QROWS, WIDTH), BF16),
            pltpu.VMEM((2, X, X_LEVELS, QROWS, WIDTH), BF16),
            pltpu.VMEM((2, QROWS, WIDTH), BF16),
            pltpu.VMEM((Y, 2, QROWS, WIDTH), BF16),
            pltpu.VMEM((Y_LEVELS, 2, QROWS, WIDTH), BF16),
            pltpu.VMEM((2, X, Y_LEVELS, QROWS, WIDTH), BF16),
            pltpu.VMEM((X_LEVELS * HALF, WIDTH), BF16),
            pltpu.VMEM((NT, TILE, X_LEVELS * HALF), BF16),
            dma((6,)),
            dma((2 * Z,)),
            dma((2 * Z,)),
            dma((Z,)),
            dma((Z,)),
            dma((Z + 1,)),
            dma((Z + 1,)),
            dma((1,)),
            dma((1,)),
            dma((X,)),
            dma((X,)),
            dma((2 * X,)),
            dma((2 * X,)),
            dma((Y,)),
            dma((Y,)),
            dma((Y_LEVELS * 2 * X,)),
            dma((Y_LEVELS * 2 * X,)),
            dma((X,)),
            dma((X,)),
            dma((Y,)),
            dma((Y,)),
            pltpu.SemaphoreType.REGULAR((2,)),
            dma((1,)),
            dma((1,)),
        ],
        compiler_params=pltpu.CompilerParams(
            collective_id=0, has_side_effects=True, vmem_limit_bytes=40 * 1024 * 1024
        ),
        name="blocks_and_states",
    )(*[pltpu.with_memory_space_constraint(a, pltpu.HBM) for a in arguments])
    return pl.pallas_call(
        last,
        out_shape=jax.ShapeDtypeStruct((tokens, width), BF16),
        in_specs=[vmem] * 3,
        out_specs=pl.BlockSpec(memory_space=pltpu.HBM),
        scratch_shapes=[pltpu.VMEM((tokens, width), BF16), dma((NT,))],
        compiler_params=pltpu.CompilerParams(vmem_limit_bytes=16 * 1024 * 1024),
        name="rows_before",
    )(near, qy, by)


def solution(mesh):
    in_specs = (P("seq", "head"), P("seq", "head"), P("seq", "head"), P(), P("seq"), P("seq"))
    out_specs = P("seq", "head")
    return jax.shard_map(local, mesh=mesh, in_specs=in_specs, out_specs=out_specs, check_vma=False)
```

```python
import jax
import jax.numpy as jnp
from jax import lax
from jax.experimental import pallas as pl
from jax.experimental.pallas import tpu as pltpu
from jax.sharding import PartitionSpec as P

MESH = pl.DeviceIdType.MESH
F32 = jnp.float32
BF16 = jnp.bfloat16

X = 4
Y = 8
Z = 8
TILE = 256
NT = 8
HALF = 128
WIDTH = 256
NEAR_LEVELS = 9
MID_LEVELS = 3
X_LEVELS = 2
Y_LEVELS = 3
FAR_LEVELS = X_LEVELS + Y_LEVELS
LANE = 64
QROWS = 16
TAG = 16
TWO_HOPS = (2, 6, 1, 7)
FARTHEST_FIRST = (4, 3, 5, 2, 6, 1, 7)
DIM0 = (((0,), (0,)), ((), ()))


def dot(a, b):
    return jnp.dot(a, b, preferred_element_type=F32)


def same(a, b):
    return jnp.where(a == b, 1.0, 0.0).astype(F32)


def body(
    k_hbm,
    q_hbm,
    v_hbm,
    tab_hbm,
    cls_hbm,
    doc_hbm,
    near,
    qy,
    by,
    tab_ref,
    cls_ref,
    doc_ref,
    v,
    v_beside,
    kg,
    qg,
    onehot,
    table,
    grid,
    scale,
    kt,
    state,
    left9,
    left10,
    left11,
    tails,
    xtag,
    ytag,
    xbuf,
    xlow,
    xout,
    ysend,
    ybuf,
    ylow,
    yout,
    bx,
    qx,
    in_sem,
    ks_sem,
    kr_sem,
    kps_sem,
    kpr_sem,
    qs_sem,
    qr_sem,
    qps_sem,
    qpr_sem,
    xs_sem,
    xr_sem,
    as_sem,
    ar_sem,
    ys_sem,
    yr_sem,
    bs_sem,
    br_sem,
    ts_sem,
    tr_sem,
    us_sem,
    ur_sem,
    ready_sem,
    vs_sem,
    vr_sem,
):
    seq = lax.axis_index("seq")
    head = lax.axis_index("head")
    x = lax.rem(seq, X)
    y = lax.div(seq, X)
    z = lax.div(head, 2)
    c = lax.rem(head, 2)

    def at_z(d):
        return {"seq": seq, "head": lax.rem(z + d, Z) * 2 + c}

    def at_x(d):
        return {"seq": y * X + lax.rem(x + d, X), "head": head}

    def beside_x(d):
        return {"seq": y * X + lax.rem(x + d, X), "head": z * 2 + (1 - c)}

    def at_y(row):
        return {"seq": row * X + x, "head": head}

    partner = {"seq": seq, "head": z * 2 + (1 - c)}

    def remote(src, dst, send, recv, device):
        return pltpu.make_async_remote_copy(
            src_ref=src,
            dst_ref=dst,
            send_sem=send,
            recv_sem=recv,
            device_id=device,
            device_id_type=MESH,
        )

    barrier = pltpu.get_barrier_semaphore()
    peers = [at_z(d) for d in TWO_HOPS] + [at_x(d) for d in (2, 1, 3)]
    peers = peers + [at_y(lax.rem(y + d, Y)) for d in TWO_HOPS]
    peers = peers + [partner]
    for peer in peers:
        pl.semaphore_signal(barrier, inc=1, device_id=peer, device_id_type=MESH)

    load_k = pltpu.make_async_copy(k_hbm, kg.at[c, z], in_sem.at[0])
    load_q = pltpu.make_async_copy(q_hbm, qg.at[c, z], in_sem.at[1])
    load_v = pltpu.make_async_copy(v_hbm, v, in_sem.at[2])
    load_k.start()
    load_q.start()
    small_loads = [
        pltpu.make_async_copy(tab_hbm, tab_ref, in_sem.at[3]),
        pltpu.make_async_copy(cls_hbm, cls_ref, in_sem.at[4]),
        pltpu.make_async_copy(doc_hbm, doc_ref, in_sem.at[5]),
    ]
    for load in small_loads:
        load.start()
    load_v.start()

    pl.semaphore_wait(barrier, len(peers))

    def gather(shard, slots, send, recv):
        def own(d):
            return remote(shard, slots.at[c, z], send.at[d], recv.at[d], at_z(d))

        def onward(back, hop, index, part):
            slot = slots.at[c, lax.rem(z + Z - back, Z), :, part]
            return remote(slot, slot, send.at[index], recv.at[index], at_z(hop))

        steps = {d: own(d) for d in TWO_HOPS}
        steps[3] = onward(2, 1, 3, pl.ds(0, 1024))
        steps[5] = onward(6, 7, 5, pl.ds(0, 1024))
        steps[4] = onward(2, 2, 4, pl.ds(0, 512))
        steps[8] = onward(6, 6, 8, pl.ds(512, 512))
        return steps

    def half(h):
        return pl.ds(512 * h, 512)

    def k_own(d, h):
        slot = kg.at[c, z, :, half(h)]
        index = 2 * d + h
        return remote(k_hbm.at[:, half(h)], slot, ks_sem.at[index], kr_sem.at[index], at_z(d))

    def k_onward(back, hop, d, h):
        slot = kg.at[c, lax.rem(z + Z - back, Z), :, half(h)]
        index = 2 * d + h
        return remote(slot, slot, ks_sem.at[index], kr_sem.at[index], at_z(hop))

    k_steps = {(d, h): k_own(d, h) for d in TWO_HOPS for h in range(2)}
    for h in range(2):
        k_steps[3, h] = k_onward(2, 1, 3, h)
        k_steps[5, h] = k_onward(6, 7, 5, h)
    k_steps[4, 0] = k_onward(2, 2, 4, 0)
    k_steps[4, 1] = k_onward(6, 6, 4, 1)
    q_steps = gather(q_hbm, qg, qs_sem, qr_sem)
    for step in ((2, 0), (6, 1), (2, 1), (6, 0), (1, 0), (7, 1), (1, 1), (7, 0)):
        k_steps[step].start()

    def k_partner(d):
        slot = kg.at[c, lax.rem(z + Z - d, Z)]
        return remote(slot, slot, kps_sem.at[d], kpr_sem.at[d], partner)

    v_across = remote(v_hbm, v_beside, vs_sem.at[0], vr_sem.at[0], partner)
    v_across.start()
    load_k.wait()
    k_partner(0).start()
    for d in (2, 6):
        row = lax.rem(y + d, Y)
        pl.semaphore_signal(
            ready_sem.at[d // 4], inc=1, device_id=at_y(row), device_id_type=MESH
        )
    for load in small_loads:
        load.wait()
    load_q.wait()

    def last_doc(i):
        return doc_ref[2 * i + 1 : 2 * i + 2, HALF - 1 : HALF].astype(F32)

    xtag[x] = jnp.broadcast_to(last_doc(NT - 1), (TAG, HALF)).astype(BF16)
    t_copies = {}
    for d in (2, 1, 3):
        t_copies[d] = remote(xtag.at[x], xtag.at[x], ts_sem.at[d], tr_sem.at[d], at_x(d))
        t_copies[d].start()

    for order, level in enumerate(list(range(NEAR_LEVELS)) + [None] + list(range(NEAR_LEVELS, 17))):
        columns = slice(order * HALF, (order + 1) * HALF)
        if level is None:
            row = lax.broadcasted_iota(jnp.int32, (32, HALF), 0)
            table[:, columns] = jnp.where(row == 24, 1.0, 0.0).astype(BF16)
        else:
            weight = jnp.broadcast_to(tab_ref[:, level : level + 1], (8, HALF))
            high = weight.astype(BF16).astype(F32)
            middle = (weight - high).astype(BF16).astype(F32)
            low = weight - high - middle
            parts = [high, middle, low, jnp.zeros_like(low)]
            table[:, columns] = jnp.concatenate(parts, axis=0).astype(BF16)

    def doc_row(block):
        return doc_ref[pl.ds(block, 1), :].astype(F32)

    def doc_tile(i):
        return jnp.concatenate([doc_row(2 * i), doc_row(2 * i + 1)], axis=1)

    first_doc = doc_ref[0:1, 0:1].astype(F32)

    def grid_tile(i):
        row8 = lax.broadcasted_iota(jnp.int32, (8, TILE), 0)
        classes = jnp.concatenate(
            [cls_ref[pl.ds(2 * i, 1), :], cls_ref[pl.ds(2 * i + 1, 1), :]], axis=1
        )
        hot = jnp.where(row8 == classes, 1.0, 0.0).astype(F32)
        docs = jnp.where(row8 == 0, doc_tile(i), 0.0)
        onehot[i] = jnp.concatenate([hot, hot, hot, docs], axis=0).astype(BF16)
        wide = lax.dot_general(
            onehot[i], table[:, : 10 * HALF], DIM0, preferred_element_type=F32
        )
        t_pos = lax.broadcasted_iota(jnp.int32, (HALF, HALF), 0)
        s_pos = lax.broadcasted_iota(jnp.int32, (HALF, HALF), 1)
        apart = t_pos ^ s_pos
        causal = s_pos <= t_pos
        for a in range(2):
            rows = slice(a * HALF, (a + 1) * HALF)
            doc_t = wide[rows, 9 * HALF : 10 * HALF]
            weight = wide[rows, :HALF]
            for level in range(1, 8):
                column = wide[rows, level * HALF : (level + 1) * HALF]
                weight = jnp.where(apart >= 1 << (level - 1), column, weight)
            allowed = causal & (doc_t == doc_row(2 * i + a))
            grid[i, rows, rows] = jnp.where(allowed, weight, 0.0)
            if a == 1:
                weight = wide[rows, 8 * HALF : 9 * HALF]
                grid[i, rows, :HALF] = jnp.where(doc_t == doc_row(2 * i), weight, 0.0)
            else:
                grid[i, rows, HALF:] = jnp.zeros((HALF, HALF), F32)
        wide = lax.dot_general(
            onehot[i], table[:, 9 * HALF :], DIM0, preferred_element_type=F32
        )
        doc_t = wide[:, :HALF]
        for b in range(MID_LEVELS + FAR_LEVELS):
            weight = wide[:, (1 + b) * HALF : (2 + b) * HALF]
            if b < MID_LEVELS:
                end = jnp.maximum((i >> b << b) - 1, 0)
                end_doc = doc_row(2 * end + 1)[:, HALF - 1 : HALF]
                present = jnp.where((i >> b) % 2 == 1, 1.0, 0.0).astype(F32)
                weight = jnp.where(doc_t == end_doc, weight * present, 0.0)
            else:
                weight = jnp.where(doc_t == first_doc, weight, 0.0)
            scale[i, :, b * HALF : (b + 1) * HALF] = weight

    @pl.loop(0, NT // 2)
    def _(i):
        grid_tile(i)

    onwards = {(2, 0): [(4, 0), (3, 0)], (6, 1): [(4, 1), (5, 1)], (2, 1): [(3, 1)], (6, 0): [(5, 0)]}
    for step, following in onwards.items():
        k_steps[step].wait_recv()
        for other in following:
            k_steps[other].start()
    k_partner(2).start()
    k_partner(6).start()
    for d in (1, 7):
        for h in range(2):
            k_steps[d, h].wait_recv()
        k_partner(d).start()

    for d in TWO_HOPS:
        q_steps[d].start()
    for d in (1, 3, 2):
        t_copies[d].wait_recv()
    ytag[y] = xtag[X - 1]
    for side in range(2):
        pl.semaphore_wait(ready_sem.at[side], 1)

    def u_copy(d):
        row = lax.rem(y + d, Y)
        return remote(ytag.at[y], ytag.at[y], us_sem.at[d], ur_sem.at[d], at_y(row))

    for d in FARTHEST_FIRST:

        @pl.when(y + d < Y)
        def _():
            u_copy(d).start()

    @pl.loop(NT // 2, NT)
    def _(i):
        grid_tile(i)

    by[...] = jnp.zeros_like(by)
    load_v.wait()
    for d in (3, 5, 4):
        for h in range(2):
            k_steps[d, h].wait_recv()
        k_partner(d).start()
    v_across.wait_recv()
    end_doc = last_doc(NT - 1)
    mine = jnp.zeros((LANE, WIDTH), F32)
    theirs = jnp.zeros((LANE, WIDTH), F32)
    for a in range(2):
        keys = kg[c].astype(F32)[:, 8 * a : 8 * a + 8, :]
        docs = jnp.concatenate([doc_row(8 * a + i) for i in range(8)], axis=1)
        kept = jnp.where(docs == end_doc, keys.reshape(LANE, 1024), 0.0).astype(BF16)
        mine = mine + dot(kept, v[a * 1024 : (a + 1) * 1024, :])
        theirs = theirs + dot(kept, v_beside[a * 1024 : (a + 1) * 1024, :])
    for p in range(X):
        tails[p, c] = mine[p * QROWS : (p + 1) * QROWS].astype(BF16)
        tails[p, 1 - c] = theirs[p * QROWS : (p + 1) * QROWS].astype(BF16)

    x_copies = {}
    for d in (2, 1, 3):
        x_copies[d] = remote(
            tails.at[lax.rem(x + d, X)], xbuf.at[x], xs_sem.at[d], xr_sem.at[d], at_x(d)
        )
        x_copies[d].start()
    xbuf[x] = tails[x]
    for d, first, second in ((2, 3, 4), (6, 5, 8)):
        q_steps[d].wait_recv()
        q_steps[first].start()
        q_steps[second].start()

    for d in (0, 2, 6, 1, 7, 3, 5, 4):
        k_partner(d).wait_recv()

    def unpacked(gathered, j):
        wide = gathered[:, :, :, pl.ds(pl.multiple_of(j * TILE, TILE), TILE)].astype(F32)
        return [wide[:, :, 8 * a : 8 * a + 8, :].reshape(HALF, TILE) for a in range(2)]

    @pl.loop(0, NT // 2)
    def _(j):
        for a, keys in enumerate(unpacked(kg, j)):
            i = a * (NT // 2) + j
            docs = doc_tile(i)
            kept = jnp.where(docs == docs[:, TILE - 1 : TILE], keys, 0.0)
            kt[i] = keys.astype(BF16)
            part = dot(kept.astype(BF16), v[pl.ds(pl.multiple_of(i * TILE, TILE), TILE), :])
            state[i] = part
            left9[i] = part.astype(BF16)

    level_states = [state[i] for i in range(NT)]
    pairs = [
        level_states[2 * j + 1] + same(last_doc(2 * j), last_doc(2 * j + 1)) * level_states[2 * j]
        for j in range(4)
    ]
    for j in range(4):
        left10[j] = pairs[j].astype(BF16)
    first_quad = pairs[1] + same(last_doc(1), last_doc(3)) * pairs[0]
    left11[...] = first_quad.astype(BF16)

    for d in (1, 3, 2):
        x_copies[d].wait_recv()
    ends = [xtag[p].astype(F32)[0:1, 0:1] for p in range(X)]
    terms = [xbuf[p].astype(F32) for p in range(X)]
    low_pair = terms[1] + same(ends[0], ends[1]) * terms[0]
    high_pair = terms[3] + same(ends[2], ends[3]) * terms[2]
    row_tail = high_pair + same(ends[1], ends[3]) * low_pair
    ysend[...] = row_tail.astype(BF16)

    def y_copy(d):
        row = lax.rem(y + d, Y)
        return remote(ysend, ybuf.at[y], ys_sem.at[d], yr_sem.at[d], at_y(row))

    for d in FARTHEST_FIRST:

        @pl.when(y + d < Y)
        def _():
            y_copy(d).start()

    blank = jnp.zeros((2, QROWS, WIDTH), BF16)
    low = low_pair.astype(BF16)
    pieces = [(blank, blank), (xbuf[0], blank), (blank, low), (xbuf[2], low)]
    for p in range(X):
        for b in range(X_LEVELS):
            for core in range(2):
                xlow[p, core, b] = pieces[p][b][core]

    def fan_out(make):
        return [make(d, d, at_x(d), c) for d in (2, 1, 3)] + [
            make(d, X + d, beside_x(d), 1 - c) for d in (2, 1, 3, 0)
        ]

    def a_copy(d, index, device, core):
        source = xlow.at[lax.rem(x + d, X), core]
        return remote(source, xout.at[c, x], as_sem.at[index], ar_sem.at[index], device)

    a_copies = fan_out(a_copy)
    for copy in a_copies:
        copy.start()
    xout[c, x] = xlow[x, c]

    for d in (1, 7, 3, 5, 4, 8):
        q_steps[d].wait_recv()
    q_partner = remote(qg.at[c], qg.at[c], qps_sem.at[0], qpr_sem.at[0], partner)
    q_partner.start()

    q_partner.wait_recv()

    def near_tile(i, queries):
        turned = queries.T
        rows = pl.ds(pl.multiple_of(i * TILE, TILE), TILE)
        scores = dot(turned.astype(BF16), kt[i])
        weighted = (scores * grid[i]).astype(BF16)
        total = dot(weighted, v[rows, :])
        mids = []
        for b in range(MID_LEVELS):
            mids.append((scale[i, :, b * HALF : (b + 1) * HALF] * turned).astype(BF16))
        lefts = [
            left9[jnp.maximum(i - 1, 0)],
            left10[jnp.maximum((i >> 1) - 1, 0)],
            left11[...],
        ]
        total = total + dot(jnp.concatenate(mids, axis=1), jnp.concatenate(lefts, axis=0))
        near[i] = total
        for b in range(FAR_LEVELS):
            start = (MID_LEVELS + b) * HALF
            target, place = (qx, b) if b < X_LEVELS else (qy, b - X_LEVELS)
            columns = slice(place * HALF, (place + 1) * HALF)
            target[i, :, columns] = (scale[i, :, start : start + HALF] * turned).astype(BF16)

    @pl.loop(0, NT // 4)
    def _(j):
        for a, queries in enumerate(unpacked(qg, j)):
            near_tile(a * (NT // 2) + j, queries)

    for d in range(1, Y):

        @pl.when(y >= d)
        def _():
            u_copy(d).wait_recv()

    def y_row(row):
        return ybuf[row].astype(F32)

    def y_end(row):
        return ytag[row].astype(F32)[0:1, 0:1]

    def b_copies(b):
        def b_copy(d, index, device, core):
            send, recv = bs_sem.at[b * 2 * X + index], br_sem.at[b * 2 * X + index]
            return remote(ylow.at[b, core], yout.at[c, x, b], send, recv, device)

        return fan_out(b_copy)

    def hand_on(b, merged):
        ylow[b] = merged
        for copy in b_copies(b):
            copy.start()
        yout[c, x, b] = ylow[b, c]

    bits = [lax.rem(y, 2) == 1, lax.rem(lax.div(y, 2), 2) == 1, y >= 4]
    four = lax.div(y, 4) * 4

    @pl.when(bits[0])
    def _():
        y_copy(1).wait_recv()
        hand_on(0, ybuf[y - 1])

    @pl.when(bits[1])
    def _():
        for d in range(2):
            y_copy(y - four - d).wait_recv()
        merged = y_row(four + 1) + same(y_end(four), y_end(four + 1)) * y_row(four)
        hand_on(1, merged.astype(BF16))

    @pl.when(bits[2])
    def _():
        for d in range(4):
            y_copy(y - d).wait_recv()
        early = y_row(1) + same(y_end(0), y_end(1)) * y_row(0)
        late = y_row(3) + same(y_end(2), y_end(3)) * y_row(2)
        merged = late + same(y_end(1), y_end(3)) * early
        hand_on(2, merged.astype(BF16))

    for copy in a_copies:
        copy.wait_recv()
    before = xtag[jnp.maximum(x - 1, 0)].astype(F32)[0:1, 0:1]
    x_masks = [same(before, first_doc), same(ends[1], first_doc)]
    for b in range(2):
        rows = xout[:, :, b].astype(F32).reshape(HALF, WIDTH)
        bx[b * HALF : (b + 1) * HALF] = (rows * x_masks[b]).astype(BF16)

    @pl.loop(NT // 4, NT // 2)
    def _(j):
        for a, queries in enumerate(unpacked(qg, j)):
            near_tile(a * (NT // 2) + j, queries)
        for done in (j - NT // 4, j + NT // 4, j, j + NT // 2):
            near[done] = near[done] + dot(qx[done], bx[...])

    y_ends = [y - 1, four + 1, 3]
    for b in range(Y_LEVELS):

        @pl.when(bits[b])
        def _():
            for copy in b_copies(b):
                copy.wait_recv()
            rows = yout[:, :, b].astype(F32).reshape(HALF, WIDTH)
            mask = same(y_end(y_ends[b]), first_doc)
            by[b * HALF : (b + 1) * HALF] = (rows * mask).astype(BF16)

    for step in k_steps:
        k_steps[step].wait_send()
    for step in q_steps:
        q_steps[step].wait_send()
    for d in range(Z):
        k_partner(d).wait_send()
    q_partner.wait_send()
    v_across.wait_send()
    for d in range(1, X):
        t_copies[d].wait_send()
        x_copies[d].wait_send()
    for copy in a_copies:
        copy.wait_send()
    for b in range(Y_LEVELS):

        @pl.when(bits[b])
        def _():
            for copy in b_copies(b):
                copy.wait_send()

    for d in range(1, Y):

        @pl.when(y + d < Y)
        def _():
            u_copy(d).wait_send()
            y_copy(d).wait_send()


def last(near, qy, by, out_hbm, out, out_sem):
    copies = []
    for i in range(NT):
        rows = pl.ds(i * TILE, TILE)
        out[rows, :] = (near[i] + dot(qy[i], by[...])).astype(BF16)
        copies.append(pltpu.make_async_copy(out.at[rows], out_hbm.at[rows], out_sem.at[i]))
        copies[i].start()
    for copy in copies:
        copy.wait()


def folded(shard):
    tokens, width = shard.shape
    return shard.T.reshape(width, 2, tokens // 2).swapaxes(0, 1).reshape(2 * width, tokens // 2)


def local(queries, key_vectors, values, level_table, level_class, doc_ids):
    tokens, width = values.shape
    vmem = pl.BlockSpec(memory_space=pltpu.VMEM)
    hbm = pl.BlockSpec(memory_space=pltpu.HBM)
    dma = pltpu.SemaphoreType.DMA
    arguments = (
        folded(key_vectors),
        folded(queries),
        values,
        level_table,
        level_class.reshape(tokens // HALF, HALF),
        doc_ids.reshape(tokens // HALF, HALF),
    )
    near, qy, by = pl.pallas_call(
        body,
        out_shape=[
            pltpu.VMEM((NT, TILE, WIDTH), F32),
            pltpu.VMEM((NT, TILE, Y_LEVELS * HALF), BF16),
            pltpu.VMEM((Y_LEVELS * HALF, WIDTH), BF16),
        ],
        in_specs=[hbm] * 6,
        out_specs=[vmem] * 3,
        scratch_shapes=[
            pltpu.VMEM(level_table.shape, F32),
            pltpu.VMEM((tokens // HALF, HALF), jnp.int32),
            pltpu.VMEM((tokens // HALF, HALF), jnp.int32),
            pltpu.VMEM((tokens, width), BF16),
            pltpu.VMEM((tokens, width), BF16),
            pltpu.VMEM((2, Z, 16, tokens // 2), BF16),
            pltpu.VMEM((2, Z, 16, tokens // 2), BF16),
            pltpu.VMEM((NT, 32, TILE), BF16),
            pltpu.VMEM((32, 18 * HALF), BF16),
            pltpu.VMEM((NT, TILE, TILE), F32),
            pltpu.VMEM((NT, TILE, (MID_LEVELS + FAR_LEVELS) * HALF), F32),
            pltpu.VMEM((NT, HALF, TILE), BF16),
            pltpu.VMEM((NT, HALF, WIDTH), F32),
            pltpu.VMEM((NT, HALF, WIDTH), BF16),
            pltpu.VMEM((4, HALF, WIDTH), BF16),
            pltpu.VMEM((HALF, WIDTH), BF16),
            pltpu.VMEM((X, 2, QROWS, WIDTH), BF16),
            pltpu.VMEM((X, TAG, HALF), BF16),
            pltpu.VMEM((Y, TAG, HALF), BF16),
            pltpu.VMEM((X, 2, QROWS, WIDTH), BF16),
            pltpu.VMEM((X, 2, X_LEVELS, QROWS, WIDTH), BF16),
            pltpu.VMEM((2, X, X_LEVELS, QROWS, WIDTH), BF16),
            pltpu.VMEM((2, QROWS, WIDTH), BF16),
            pltpu.VMEM((Y, 2, QROWS, WIDTH), BF16),
            pltpu.VMEM((Y_LEVELS, 2, QROWS, WIDTH), BF16),
            pltpu.VMEM((2, X, Y_LEVELS, QROWS, WIDTH), BF16),
            pltpu.VMEM((X_LEVELS * HALF, WIDTH), BF16),
            pltpu.VMEM((NT, TILE, X_LEVELS * HALF), BF16),
            dma((6,)),
            dma((2 * Z,)),
            dma((2 * Z,)),
            dma((Z,)),
            dma((Z,)),
            dma((Z + 1,)),
            dma((Z + 1,)),
            dma((1,)),
            dma((1,)),
            dma((X,)),
            dma((X,)),
            dma((2 * X,)),
            dma((2 * X,)),
            dma((Y,)),
            dma((Y,)),
            dma((Y_LEVELS * 2 * X,)),
            dma((Y_LEVELS * 2 * X,)),
            dma((X,)),
            dma((X,)),
            dma((Y,)),
            dma((Y,)),
            pltpu.SemaphoreType.REGULAR((2,)),
            dma((1,)),
            dma((1,)),
        ],
        compiler_params=pltpu.CompilerParams(
            collective_id=0, has_side_effects=True, vmem_limit_bytes=40 * 1024 * 1024
        ),
        name="blocks_and_states",
    )(*[pltpu.with_memory_space_constraint(a, pltpu.HBM) for a in arguments])
    return pl.pallas_call(
        last,
        out_shape=jax.ShapeDtypeStruct((tokens, width), BF16),
        in_specs=[vmem] * 3,
        out_specs=pl.BlockSpec(memory_space=pltpu.HBM),
        scratch_shapes=[pltpu.VMEM((tokens, width), BF16), dma((NT,))],
        compiler_params=pltpu.CompilerParams(vmem_limit_bytes=16 * 1024 * 1024),
        name="rows_before",
    )(near, qy, by)


def solution(mesh):
    in_specs = (P("seq", "head"), P("seq", "head"), P("seq", "head"), P(), P("seq"), P("seq"))
    out_specs = P("seq", "head")
    return jax.shard_map(local, mesh=mesh, in_specs=in_specs, out_specs=out_specs, check_vma=False)
```
